256 devices in a mesh: space: 16 (over z, core), tm: 16 (over y, x).
Axes of the slice: x: 4, y: 4, z: 8, core: 2. Of those that a mesh axis runs over, the one named last changes fastest.
Arguments:
- snapshots: bfloat16 [131072, 4096], P('space', 'tm'), may hold values from -6 to 6
- pod_basis: bfloat16 [131072, 512], P('space'), may hold values from -0.015625 to 0.015625
Outputs:
- hankel_gram: float32 [4096, 4096], P('tm', 'space')
The draws below stay inside these ranges and needn't reach their ends.
All inputs are finite; a program needn't handle non-finite values.
Results may differ from the reference program's by a relative error of at most 0.0014.
Values may be sent and summed in bfloat16 or wider, within the bound.
A program may use at most 64 MiB of HBM per device.

```python
import jax
import jax.numpy as jnp

MODES = 512
DELAYS = 64
POINTS = 131072
STEPS = 4096


def steps_of(own_key, shape, split, least, largest):
    loudness = 1.0
    for axis_at, shards_of in split:
        draws = jax.random.uniform(jax.random.fold_in(jax.random.fold_in(own_key, 6), axis_at), (shards_of,), jnp.float32, least / len(split), largest / len(split))
        loudness = loudness * jnp.repeat(jnp.exp(draws), shape[axis_at] // shards_of).reshape((-1,) + (1,) * (len(shape) - 1 - axis_at))
    return loudness


def gaussian(stream_key, shape, deviation, bound, cuts=(), dtype=jnp.bfloat16):
    drawn = jax.random.normal(stream_key, shape, jnp.float32) * deviation
    if len(cuts) > 0:
        drawn = steps_of(stream_key, shape, cuts, -0.22, 0.18) * drawn
    return jnp.clip(drawn, min=-bound, max=bound).astype(dtype)


def setup_inputs(seed: int = 0) -> dict:
    splits = jax.random.split(jax.random.key(seed), 3)
    return {
        "snapshots": gaussian(splits[0], (POINTS, STEPS), 1.0, 6.0, ((0, 16), (1, 16))),
        "pod_basis": gaussian(splits[1], (POINTS, MODES), POINTS ** -0.5, 0.015625, ((0, 16),)),
    }


def reference(snapshots, pod_basis):
    coeffs = jnp.dot(pod_basis.T, snapshots, preferred_element_type=jnp.float32).astype(jnp.bfloat16)
    padded = jnp.concatenate([coeffs, jnp.zeros((MODES, DELAYS), jnp.bfloat16)], axis=1)
    kernel = jnp.dot(padded.T, padded, preferred_element_type=jnp.float32)
    total = jnp.zeros((STEPS, STEPS), jnp.float32)
    for offset in range(DELAYS):
        total = total + kernel[offset:offset + STEPS, offset:offset + STEPS]
    return total * ((MODES * DELAYS) ** -0.5)
```

```python
import jax
import jax.numpy as jnp
from jax import lax
from jax.experimental import pallas as pl
from jax.experimental.pallas import tpu as pltpu
from jax.sharding import PartitionSpec as P

MODES = 512
DELAYS = 64
MESH = pl.DeviceIdType.MESH
NZ = 8
NT = 16
STEPS = 256
POINTS = 8192
HALF = 256
PIECES = MODES // HALF
CHUNK = 16
OWN = STEPS // 2
KCUT = 4
KC = POINTS // KCUT
ROWS = STEPS + DELAYS
COLS = 384
SCALE = (MODES * DELAYS) ** -0.5


def kernel(
    snap,
    pod,
    out,
    sv,
    pv,
    acc,
    sib_buf,
    mine,
    rs_buf,
    ci,
    cj,
    s_sem,
    p_sem,
    sib_ss,
    sib_rs,
    rs_ss,
    rs_rs,
    za_ss,
    za_rs,
    sw_ss,
    sw_rs,
    rh_ss,
    rh_rs,
    fw_ss,
    fw_rs,
    sc_ss,
    sc_rs,
    hs_ss,
    hs_rs,
    ag_ss,
    ag_rs,
    ah_ss,
    ah_rs,
):
    space = lax.axis_index("space")
    tm = lax.axis_index("tm")
    z = space // 2
    core = lax.rem(space, 2)
    chunk_at = core * NZ + z

    sibling = {"space": z * 2 + 1 - core, "tm": tm}

    def z_peer(d):
        return {"space": lax.rem(z + d, NZ) * 2 + core, "tm": tm}

    def plane_peer(d):
        return {"space": space, "tm": lax.rem(tm + d, NT)}

    def owner_space(k):
        return lax.rem(k, NZ) * 2 + k // NZ

    scatter_to = {"space": tm, "tm": chunk_at}
    scatter_from = {"space": owner_space(tm), "tm": space}
    scatter_self = jnp.logical_and(chunk_at == tm, space == tm)
    odd_plane = lax.rem(space, 2)
    halo_owner = jnp.logical_and(chunk_at < 4, tm >= 1)
    halo_plane = lax.rem(tm + NT - 1, NT)
    halo_to = {
        "space": halo_plane,
        "tm": jnp.where(lax.rem(halo_plane, 2) == 0, 5 * chunk_at, 3 * chunk_at + 3)
        * jnp.where(halo_owner, 1, 0),
    }
    holds_even = jnp.logical_and(odd_plane == 0, lax.rem(tm, 5) == 0)
    holds_odd = jnp.logical_and(
        odd_plane == 1,
        jnp.logical_and(lax.rem(tm, 3) == 0, jnp.logical_and(tm >= 3, tm <= 12)),
    )
    has_next = space < NT - 1
    holder = jnp.logical_and(has_next, jnp.logical_or(holds_even, holds_odd))
    held_halo = jnp.where(
        holder, jnp.where(odd_plane == 0, tm // 5, tm // 3 - 1), 0
    )
    halo_from = {"space": held_halo * 2, "tm": lax.rem(space + 1, NT)}

    for k in range(KCUT):
        at = pl.ds(k * KC, KC)
        pltpu.make_async_copy(snap.at[at], sv.at[at], s_sem.at[k]).start()
        pltpu.make_async_copy(
            pod.at[at, pl.ds(0, HALF)], pv.at[0, at], p_sem.at[0, k]
        ).start()
    for p in range(1, PIECES):
        for k in range(KCUT):
            at = pl.ds(k * KC, KC)
            pltpu.make_async_copy(
                pod.at[at, pl.ds(p * HALF, HALF)], pv.at[p, at], p_sem.at[p, k]
            ).start()

    barrier = pltpu.get_barrier_semaphore()

    def greet(who):
        pl.semaphore_signal(barrier, inc=1, device_id=who, device_id_type=MESH)

    greet(sibling)
    for d in range(1, NZ):
        greet(z_peer(d))
    for d in range(1, NT):
        greet(plane_peer(d))

    @pl.when(jnp.logical_not(scatter_self))
    def _():
        greet(scatter_from)

    @pl.when(holder)
    def _():
        greet(halo_from)

    expected = (
        1
        + (NZ - 1)
        + (NT - 1)
        + jnp.where(scatter_self, 0, 1)
        + jnp.where(halo_owner, 1, 0)
    )

    cj[:, ROWS:, :] = jnp.zeros((PIECES, COLS - ROWS, HALF), jnp.bfloat16)

    @pl.when(space == NT - 1)
    def _():
        cj[:, STEPS:ROWS, :] = jnp.zeros((PIECES, DELAYS, HALF), jnp.bfloat16)

    @pl.when(tm == NT - 1)
    def _():
        ci[:, STEPS:ROWS, :] = jnp.zeros((PIECES, DELAYS, HALF), jnp.bfloat16)

    def multiply(p, k):
        at = pl.ds(k * KC, KC)
        if p == 0:
            pltpu.make_async_copy(snap.at[at], sv.at[at], s_sem.at[k]).wait()
        pltpu.make_async_copy(
            pod.at[at, pl.ds(p * HALF, HALF)], pv.at[p, at], p_sem.at[p, k]
        ).wait()
        term = lax.dot_general(
            sv[at],
            pv[p, at],
            (((0,), (0,)), ((), ())),
            preferred_element_type=jnp.float32,
        )
        if k == 0:
            acc[p] = term
        else:
            acc[p] += term

    def remote(src, dst, ss, rs, who):
        return pltpu.make_async_remote_copy(
            src_ref=src,
            dst_ref=dst,
            send_sem=ss,
            recv_sem=rs,
            device_id=who,
            device_id_type=MESH,
        )

    own_rows = pl.ds(pl.multiple_of(core * OWN, OWN), OWN)
    other_rows = pl.ds(pl.multiple_of((1 - core) * OWN, OWN), OWN)
    chunk_rows = pl.ds(pl.multiple_of(chunk_at * CHUNK, CHUNK), CHUNK)
    held_rows = pl.ds(pl.multiple_of(tm * CHUNK, CHUNK), CHUNK)

    def sib_copy(p):
        return remote(
            acc.at[p, other_rows], sib_buf.at[p], sib_ss.at[p], sib_rs.at[p], sibling
        )

    def rs_copy(p, d):
        to = lax.rem(z + d, NZ)
        rows = pl.ds(pl.multiple_of(to * CHUNK, CHUNK), CHUNK)
        return remote(
            mine.at[p, rows],
            rs_buf.at[p, d - 1],
            rs_ss.at[p, d - 1],
            rs_rs.at[p, d - 1],
            z_peer(d),
        )

    def za_copy(p, d):
        return remote(
            ci.at[p, chunk_rows],
            ci.at[p, chunk_rows],
            za_ss.at[p, d - 1],
            za_rs.at[p, d - 1],
            z_peer(d),
        )

    def swap_copy(p):
        return remote(
            ci.at[p, own_rows], ci.at[p, own_rows], sw_ss.at[p], sw_rs.at[p], sibling
        )

    def row_halo_copy(p):
        return remote(
            ci.at[p, pl.ds(0, DELAYS)],
            ci.at[p, pl.ds(STEPS, DELAYS)],
            rh_ss.at[p],
            rh_rs.at[p],
            plane_peer(NT - 1),
        )

    def forward_copy(p):
        return remote(
            ci.at[p, pl.ds(STEPS, DELAYS)],
            ci.at[p, pl.ds(STEPS, DELAYS)],
            fw_ss.at[p],
            fw_rs.at[p],
            sibling,
        )

    def scatter_copy(p):
        return remote(
            ci.at[p, chunk_rows],
            cj.at[p, chunk_rows],
            sc_ss.at[p],
            sc_rs.at[p],
            scatter_to,
        )

    def halo_scatter_copy(p):
        rows = pl.ds(
            pl.multiple_of(STEPS + lax.rem(chunk_at, 4) * CHUNK, CHUNK), CHUNK
        )
        return remote(
            ci.at[p, chunk_rows], cj.at[p, rows], hs_ss.at[p], hs_rs.at[p], halo_to
        )

    def ag_copy(p, d):
        return remote(
            cj.at[p, held_rows],
            cj.at[p, held_rows],
            ag_ss.at[p, d - 1],
            ag_rs.at[p, d - 1],
            plane_peer(d),
        )

    held_halo_rows = pl.ds(
        pl.multiple_of(STEPS + held_halo * CHUNK, CHUNK), CHUNK
    )

    def ag_halo_copy(p, d):
        return remote(
            cj.at[p, held_halo_rows],
            cj.at[p, held_halo_rows],
            ah_ss.at[p, d - 1],
            ah_rs.at[p, held_halo],
            plane_peer(d),
        )

    def start_rs(p):
        sib_copy(p).wait_recv()
        mine[p] = acc[p, own_rows] + sib_buf[p]
        for d in range(1, NZ):
            rs_copy(p, d).start()

    def finish_rs(p):
        total = mine[p, pl.ds(pl.multiple_of(z * CHUNK, CHUNK), CHUNK)]
        for d in range(1, NZ):
            rs_copy(p, d).wait_recv()
            total = total + rs_buf[p, d - 1]
        rounded = total.astype(jnp.bfloat16)
        ci[p, chunk_rows] = rounded

        @pl.when(scatter_self)
        def _():
            cj[p, chunk_rows] = rounded

        @pl.when(jnp.logical_not(scatter_self))
        def _():
            scatter_copy(p).start()

        @pl.when(halo_owner)
        def _():
            halo_scatter_copy(p).start()

        for d in range(1, NZ):
            za_copy(p, d).start()

    def start_ag(p):
        @pl.when(jnp.logical_not(scatter_self))
        def _():
            scatter_copy(p).wait_recv()

        for d in range(1, NT):
            ag_copy(p, d).start()

        @pl.when(holder)
        def _():
            halo_scatter_copy(p).wait_recv()
            for d in range(1, NT):
                ag_halo_copy(p, d).start()

    def finish_za(p):
        for d in range(1, NZ):
            za_copy(p, d).wait_recv()
        swap_copy(p).start()

        @pl.when(jnp.logical_and(core == 0, tm >= 1))
        def _():
            row_halo_copy(p).start()

    def finish_row_halo(p):
        @pl.when(jnp.logical_and(core == 0, tm < NT - 1))
        def _():
            row_halo_copy(p).wait_recv()
            forward_copy(p).start()

        @pl.when(jnp.logical_and(core == 1, tm < NT - 1))
        def _():
            forward_copy(p).wait_recv()

    def finish_ag(p):
        for d in range(1, NT):
            ag_copy(p, d).wait_recv()
        for k in range(4):

            @pl.when(
                jnp.logical_and(
                    has_next, jnp.logical_not(jnp.logical_and(holder, held_halo == k))
                )
            )
            def _():
                pltpu.make_async_copy(
                    cj.at[p, pl.ds(0, CHUNK)],
                    cj.at[p, pl.ds(STEPS + k * CHUNK, CHUNK)],
                    ah_rs.at[p, k],
                ).wait()

    def gram(p):
        return lax.dot_general(
            ci[p],
            cj[p],
            (((1,), (1,)), ((), ())),
            preferred_element_type=jnp.float32,
        )

    for k in range(KCUT):
        multiply(0, k)
    pl.semaphore_wait(barrier, expected)
    sib_copy(0).start()
    multiply(1, 0)
    multiply(1, 1)
    start_rs(0)
    multiply(1, 2)
    multiply(1, 3)
    sib_copy(1).start()
    start_rs(1)
    finish_rs(0)
    finish_rs(1)
    start_ag(0)
    finish_za(0)
    start_ag(1)
    finish_za(1)
    swap_copy(0).wait_recv()
    finish_row_halo(0)
    finish_ag(0)
    total = gram(0)
    swap_copy(1).wait_recv()
    finish_row_halo(1)
    finish_ag(1)
    total = total + gram(1)
    shift = 1
    while shift < DELAYS:
        moved = pltpu.roll(total, ROWS - shift, 0)
        total = total + pltpu.roll(moved, COLS - shift, 1)
        shift *= 2
    out[...] = total[:STEPS, :STEPS] * SCALE

    for p in range(PIECES):
        sib_copy(p).wait_send()
        swap_copy(p).wait_send()
        for d in range(1, NZ):
            rs_copy(p, d).wait_send()
            za_copy(p, d).wait_send()
        for d in range(1, NT):
            ag_copy(p, d).wait_send()

        @pl.when(holder)
        def _():
            for d in range(1, NT):
                ag_halo_copy(p, d).wait_send()

        @pl.when(jnp.logical_not(scatter_self))
        def _():
            scatter_copy(p).wait_send()

        @pl.when(halo_owner)
        def _():
            halo_scatter_copy(p).wait_send()

        @pl.when(jnp.logical_and(core == 0, tm >= 1))
        def _():
            row_halo_copy(p).wait_send()

        @pl.when(jnp.logical_and(core == 0, tm < NT - 1))
        def _():
            forward_copy(p).wait_send()


def per_device(snapshots, pod_basis):
    dma = pltpu.SemaphoreType.DMA
    pairs = [
        (PIECES,),
        (PIECES, NZ - 1),
        (PIECES, NZ - 1),
        (PIECES,),
        (PIECES,),
        (PIECES,),
        (PIECES,),
        (PIECES,),
        (PIECES, NT - 1),
    ]
    sems = [dma((KCUT,)), dma((PIECES, KCUT))]
    for shape in pairs:
        sems += [dma(shape), dma(shape)]
    sems += [dma((PIECES, NT - 1)), dma((PIECES, 4))]
    return pl.pallas_call(
        kernel,
        out_shape=jax.ShapeDtypeStruct((STEPS, STEPS), jnp.float32),
        in_specs=[pl.BlockSpec(memory_space=pl.ANY)] * 2,
        out_specs=pl.BlockSpec(memory_space=pltpu.VMEM),
        scratch_shapes=[
            pltpu.VMEM((POINTS, STEPS), jnp.bfloat16),
            pltpu.VMEM((PIECES, POINTS, HALF), jnp.bfloat16),
            pltpu.VMEM((PIECES, STEPS, HALF), jnp.float32),
            pltpu.VMEM((PIECES, OWN, HALF), jnp.float32),
            pltpu.VMEM((PIECES, OWN, HALF), jnp.float32),
            pltpu.VMEM((PIECES, NZ - 1, CHUNK, HALF), jnp.float32),
            pltpu.VMEM((PIECES, ROWS, HALF), jnp.bfloat16),
            pltpu.VMEM((PIECES, COLS, HALF), jnp.bfloat16),
        ]
        + sems,
        compiler_params=pltpu.CompilerParams(
            collective_id=0, has_side_effects=True, vmem_limit_bytes=40 << 20
        ),
    )(snapshots, pod_basis)


def solution(mesh):
    in_specs = (P("space", "tm"), P("space", None))
    out_specs = P("tm", "space")
    return jax.shard_map(
        per_device, mesh=mesh, in_specs=in_specs, out_specs=out_specs, check_vma=False
    )
```

```python
import jax
import jax.numpy as jnp
from jax import lax
from jax.experimental import pallas as pl
from jax.experimental.pallas import tpu as pltpu
from jax.sharding import PartitionSpec as P

MODES = 512
DELAYS = 64
MESH = pl.DeviceIdType.MESH
NZ = 8
NT = 16
SIDE = 4
STEPS = 256
POINTS = 8192
CHUNK = 16
OWN = STEPS // 2
KCUT = 8
KC = POINTS // KCUT
ROWS = STEPS + DELAYS
COLS = 384
PIECES = 2
WIDTH = MODES // PIECES
SCALE = (MODES * DELAYS) ** -0.5
ORDER = (4, 3, 5, 2, 6, 1, 7)
NARROW = (3, 4, 5)

PLACE = {
    (4, 0): (0, 0),
    (4, 1): (1, 0),
    (3, 0): (3, 0),
    (3, 1): (0, 1),
    (5, 0): (0, 3),
    (5, 1): (1, 1),
    (2, 0): (2, 0),
    (2, 1): (0, 2),
    (6, 0): (1, 3),
    (6, 1): (3, 1),
    (1, 0): (3, 3),
    (1, 1): (2, 1),
    (7, 0): (2, 3),
    (7, 1): (1, 2),
    (0, 0): (3, 2),
    (0, 1): (2, 2),
}
DX = [PLACE[r // 2, r % 2][0] for r in range(16)]
DY = [PLACE[r // 2, r % 2][1] for r in range(16)]
PLANE = sorted(
    ((dx, dy) for dx in range(SIDE) for dy in range(SIDE) if dx or dy),
    key=lambda o: -min(o[0], SIDE - o[0]) - min(o[1], SIDE - o[1]),
)
BACK = [0] * 16
for _r in range(16):
    BACK[DY[_r] * SIDE + DX[_r]] = _r


def lookup(table, index):
    value = jnp.int32(0)
    for at, entry in enumerate(table):
        value = value + jnp.where(index == at, entry, 0)
    return value


def kernel(
    snap,
    pod,
    out,
    sv,
    pv,
    acc,
    sib_buf,
    own,
    wide_out,
    wide_in,
    narrow_out,
    narrow_in,
    ci,
    cj,
    s_sem,
    p_sem,
    sib_ss,
    sib_rs,
    rs_ss,
    rs_rs,
    za_ss,
    za_rs,
    sw_ss,
    sw_rs,
    rh_ss,
    rh_rs,
    sc_ss,
    sc_rs,
    hs_ss,
    hs_rs,
    ag_ss,
    ag_rs,
    ah_ss,
    ah_rs,
):
    space = lax.axis_index("space")
    tm = lax.axis_index("tm")
    z = space // 2
    core = lax.rem(space, 2)
    x = lax.rem(tm, SIDE)
    y = tm // SIDE
    chunk_at = core * NZ + z

    sibling = {"space": z * 2 + 1 - core, "tm": tm}

    def z_peer(d):
        return {"space": lax.rem(z + d, NZ) * 2 + core, "tm": tm}

    def plane_peer(d):
        dx, dy = PLANE[d]
        return {"space": space, "tm": lax.rem(y + dy, SIDE) * SIDE + lax.rem(x + dx, SIDE)}

    rank = lax.rem(z - tm // 2 + NZ, NZ) * 2 + core
    to_x = lax.rem(x + lookup(DX, rank), SIDE)
    to_y = lax.rem(y + lookup(DY, rank), SIDE)
    scatter_to = {"space": tm, "tm": to_y * SIDE + to_x}
    off_x = lax.rem(x - lax.rem(space, SIDE) + SIDE, SIDE)
    off_y = lax.rem(y - space // SIDE + SIDE, SIDE)
    from_rank = lookup(BACK, off_y * SIDE + off_x)
    from_z = lax.rem(z + from_rank // 2, NZ)
    from_core = lax.rem(from_rank, 2)
    held = from_core * NZ + from_z
    scatter_from = {"space": from_z * 2 + from_core, "tm": space}

    halo_owner = jnp.logical_and(chunk_at < 4, tm >= 1)
    halo_plane = lax.rem(tm + NT - 1, NT)
    halo_turn = lax.rem(lax.rem(z - halo_plane // 2 + NZ, SIDE) + 1, SIDE)
    halo_to = {"space": halo_plane, "tm": lax.rem(y + halo_turn, SIDE) * SIDE + x}
    has_next = space < NT - 1
    next_block = lax.rem(space + 1, NT)
    holder = jnp.logical_and(has_next, x == lax.rem(next_block, SIDE))
    held_turn = lax.rem(y - next_block // SIDE - 1 + 2 * SIDE, SIDE)
    held_halo = lax.rem(held_turn + z, SIDE)
    halo_from = {"space": held_halo * 2, "tm": next_block}

    sends_row_halo = jnp.logical_and(core == 0, tm >= 1)
    takes_row_halo = tm < NT - 1
    before = lax.rem(tm + NT - 1, NT)
    after = lax.rem(tm + 1, NT)

    def snap_copy(k):
        at = pl.ds(k * KC, KC)
        return pltpu.make_async_copy(snap.at[at], sv.at[at], s_sem.at[k])

    def pod_copy(k):
        at = pl.ds(k * KC, KC)
        return pltpu.make_async_copy(pod.at[at], pv.at[at], p_sem.at[k])

    for k in range(KCUT):
        snap_copy(k).start()
        pod_copy(k).start()

    barrier = pltpu.get_barrier_semaphore()

    def greet(who):
        pl.semaphore_signal(barrier, inc=1, device_id=who, device_id_type=MESH)

    greet(sibling)
    for d in range(1, NZ):
        greet(z_peer(d))
    for d in range(NT - 1):
        greet(plane_peer(d))
    greet(scatter_from)

    @pl.when(holder)
    def _():
        greet(halo_from)

    @pl.when(jnp.logical_and(core == 1, takes_row_halo))
    def _():
        greet({"space": z * 2, "tm": after})

    expected = (
        1
        + (NZ - 1)
        + (NT - 1)
        + 1
        + jnp.where(halo_owner, 1, 0)
        + jnp.where(sends_row_halo, 1, 0)
    )

    cj[:, ROWS:, :] = jnp.zeros((PIECES, COLS - ROWS, WIDTH), jnp.bfloat16)

    @pl.when(jnp.logical_not(has_next))
    def _():
        cj[:, STEPS:ROWS, :] = jnp.zeros((PIECES, DELAYS, WIDTH), jnp.bfloat16)

    @pl.when(jnp.logical_not(takes_row_halo))
    def _():
        ci[:, STEPS:ROWS, :] = jnp.zeros((PIECES, DELAYS, WIDTH), jnp.bfloat16)

    def remote(src, dst, ss, rs, who):
        return pltpu.make_async_remote_copy(
            src_ref=src,
            dst_ref=dst,
            send_sem=ss,
            recv_sem=rs,
            device_id=who,
            device_id_type=MESH,
        )

    def rows_of(start, size):
        return pl.ds(pl.multiple_of(start, CHUNK), size)

    chunk_rows = rows_of(chunk_at * CHUNK, CHUNK)
    held_rows = rows_of(held * CHUNK, CHUNK)
    held_halo_rows = rows_of(STEPS + held_halo * CHUNK, CHUNK)
    own_rows = rows_of(core * OWN, OWN)

    def sib_copy(p, d):
        to = lax.rem(z + d, NZ)
        return remote(
            acc.at[p, rows_of((1 - core) * OWN + to * CHUNK, CHUNK)],
            sib_buf.at[p, d],
            sib_ss.at[p, d],
            sib_rs.at[p, d],
            sibling,
        )

    def rs_copy(p, d):
        out_buf, in_buf = (
            (narrow_out, narrow_in) if d in NARROW else (wide_out, wide_in)
        )
        return remote(
            out_buf.at[p, d - 1],
            in_buf.at[p, d - 1],
            rs_ss.at[p, d - 1],
            rs_rs.at[p, d - 1],
            z_peer(d),
        )

    def za_copy(p, d):
        return remote(
            ci.at[p, chunk_rows],
            ci.at[p, chunk_rows],
            za_ss.at[p, d - 1],
            za_rs.at[p, d - 1],
            z_peer(d),
        )

    def swap_copy(p):
        return remote(
            ci.at[p, own_rows], ci.at[p, own_rows], sw_ss.at[p], sw_rs.at[p], sibling
        )

    def row_halo_copy(p, c):
        return remote(
            ci.at[p, pl.ds(0, DELAYS)],
            ci.at[p, pl.ds(STEPS, DELAYS)],
            rh_ss.at[p, c],
            rh_rs.at[p],
            {"space": z * 2 + c, "tm": before},
        )

    def scatter_copy(p):
        return remote(
            ci.at[p, chunk_rows],
            cj.at[p, chunk_rows],
            sc_ss.at[p],
            sc_rs.at[p],
            scatter_to,
        )

    def halo_scatter_copy(p):
        rows = rows_of(STEPS + lax.rem(z, SIDE) * CHUNK, CHUNK)
        return remote(
            ci.at[p, chunk_rows], cj.at[p, rows], hs_ss.at[p], hs_rs.at[p], halo_to
        )

    def ag_copy(p, d):
        return remote(
            cj.at[p, held_rows],
            cj.at[p, held_rows],
            ag_ss.at[p, d],
            ag_rs.at[p, d],
            plane_peer(d),
        )

    def ag_halo_copy(p, d):
        return remote(
            cj.at[p, held_halo_rows],
            cj.at[p, held_halo_rows],
            ah_ss.at[p, d],
            ah_rs.at[p, held_halo],
            plane_peer(d),
        )

    def start_sum(p):
        for d in ORDER + (0,):
            sib_copy(p, d).wait_recv()
            to = lax.rem(z + d, NZ)
            both = acc[p, rows_of(core * OWN + to * CHUNK, CHUNK)] + sib_buf[p, d]
            if d == 0:
                own[p] = both
            elif d in NARROW:
                narrow_out[p, d - 1] = both.astype(jnp.bfloat16)
            else:
                wide_out[p, d - 1] = both
            if d > 0:
                rs_copy(p, d).start()

    def finish_sum(p):
        total = own[p]
        for d in ORDER[::-1]:
            rs_copy(p, d).wait_recv()
            in_buf = narrow_in if d in NARROW else wide_in
            total = total + in_buf[p, d - 1].astype(jnp.float32)
        ci[p, chunk_rows] = total.astype(jnp.bfloat16)
        scatter_copy(p).start()

        @pl.when(halo_owner)
        def _():
            halo_scatter_copy(p).start()

        for d in ORDER:
            za_copy(p, d).start()

    def start_plane(p):
        scatter_copy(p).wait_recv()
        for d in range(NT - 1):
            ag_copy(p, d).start()

        @pl.when(holder)
        def _():
            halo_scatter_copy(p).wait_recv()
            for d in range(NT - 1):
                ag_halo_copy(p, d).start()

    def finish_z(p):
        for d in ORDER[::-1]:
            za_copy(p, d).wait_recv()
        swap_copy(p).start()

        @pl.when(sends_row_halo)
        def _():
            row_halo_copy(p, 0).start()
            row_halo_copy(p, 1).start()

    def gram(p):
        swap_copy(p).wait_recv()

        @pl.when(takes_row_halo)
        def _():
            row_halo_copy(p, 0).wait_recv()

        for d in range(NT - 1)[::-1]:
            ag_copy(p, d).wait_recv()
        for k in range(4):

            @pl.when(
                jnp.logical_and(
                    has_next, jnp.logical_not(jnp.logical_and(holder, held_halo == k))
                )
            )
            def _():
                pltpu.make_async_copy(
                    cj.at[p, pl.ds(0, CHUNK)],
                    cj.at[p, pl.ds(STEPS + k * CHUNK, CHUNK)],
                    ah_rs.at[p, k],
                ).wait()

        return lax.dot_general(
            ci[p],
            cj[p],
            (((1,), (1,)), ((), ())),
            preferred_element_type=jnp.float32,
        )

    for k in range(KCUT):
        snap_copy(k).wait()
        pod_copy(k).wait()
        at = pl.ds(k * KC, KC)
        term = lax.dot_general(
            sv[at],
            pv[at],
            (((0,), (0,)), ((), ())),
            preferred_element_type=jnp.float32,
        )
        for p in range(PIECES):
            part = term[:, p * WIDTH : (p + 1) * WIDTH]
            if k == 0:
                acc[p] = part
            else:
                acc[p] += part

    pl.semaphore_wait(barrier, expected)

    for p in range(PIECES):
        for d in ORDER + (0,):
            sib_copy(p, d).start()
    for p in range(PIECES):
        start_sum(p)
    for p in range(PIECES):
        finish_sum(p)
    for p in range(PIECES):
        start_plane(p)
        finish_z(p)

    for p in range(PIECES):
        for d in range(NZ):
            sib_copy(p, d).wait_send()
        for d in range(1, NZ):
            rs_copy(p, d).wait_send()
            za_copy(p, d).wait_send()
        scatter_copy(p).wait_send()

        @pl.when(halo_owner)
        def _():
            halo_scatter_copy(p).wait_send()

    window = gram(0)
    for p in range(1, PIECES):
        window = window + gram(p)
    shift = 1
    while shift < DELAYS:
        moved = pltpu.roll(window, ROWS - shift, 0)
        window = window + pltpu.roll(moved, COLS - shift, 1)
        shift *= 2
    out[...] = window[:STEPS, :STEPS] * SCALE

    for p in range(PIECES):
        swap_copy(p).wait_send()

        @pl.when(sends_row_halo)
        def _():
            row_halo_copy(p, 0).wait_send()
            row_halo_copy(p, 1).wait_send()

        for d in range(NT - 1):
            ag_copy(p, d).wait_send()

        @pl.when(holder)
        def _():
            for d in range(NT - 1):
                ag_halo_copy(p, d).wait_send()


def per_device(snapshots, pod_basis):
    dma = pltpu.SemaphoreType.DMA
    f32, bf16 = jnp.float32, jnp.bfloat16
    sems = [dma((KCUT,)), dma((KCUT,))]
    for sent, received in (
        ((NZ,), (NZ,)),
        ((NZ - 1,), (NZ - 1,)),
        ((NZ - 1,), (NZ - 1,)),
        ((), ()),
        ((2,), ()),
        ((), ()),
        ((), ()),
        ((NT - 1,), (NT - 1,)),
        ((NT - 1,), (4,)),
    ):
        sems += [dma((PIECES,) + sent), dma((PIECES,) + received)]
    return pl.pallas_call(
        kernel,
        out_shape=jax.ShapeDtypeStruct((STEPS, STEPS), f32),
        in_specs=[pl.BlockSpec(memory_space=pl.ANY)] * 2,
        out_specs=pl.BlockSpec(memory_space=pltpu.VMEM),
        scratch_shapes=[
            pltpu.VMEM((POINTS, STEPS), bf16),
            pltpu.VMEM((POINTS, MODES), bf16),
            pltpu.VMEM((PIECES, STEPS, WIDTH), f32),
            pltpu.VMEM((PIECES, NZ, CHUNK, WIDTH), f32),
            pltpu.VMEM((PIECES, CHUNK, WIDTH), f32),
            pltpu.VMEM((PIECES, NZ - 1, CHUNK, WIDTH), f32),
            pltpu.VMEM((PIECES, NZ - 1, CHUNK, WIDTH), f32),
            pltpu.VMEM((PIECES, NZ - 1, CHUNK, WIDTH), bf16),
            pltpu.VMEM((PIECES, NZ - 1, CHUNK, WIDTH), bf16),
            pltpu.VMEM((PIECES, ROWS, WIDTH), bf16),
            pltpu.VMEM((PIECES, COLS, WIDTH), bf16),
        ]
        + sems,
        compiler_params=pltpu.CompilerParams(
            collective_id=0, has_side_effects=True, vmem_limit_bytes=62 << 20
        ),
    )(snapshots, pod_basis)


def solution(mesh):
    in_specs = (P("space", "tm"), P("space", None))
    out_specs = P("tm", "space")
    return jax.shard_map(
        per_device, mesh=mesh, in_specs=in_specs, out_specs=out_specs, check_vma=False
    )
```

```python
import jax
import jax.numpy as jnp
from jax import lax
from jax.experimental import pallas as pl
from jax.experimental.pallas import tpu as pltpu
from jax.sharding import PartitionSpec as P

MODES = 512
DELAYS = 64
MESH = pl.DeviceIdType.MESH
NZ = 8
NT = 16
SIDE = 4
STEPS = 256
POINTS = 8192
CHUNK = 16
HALO = DELAYS // CHUNK
OWN = STEPS // 2
KCUT = 4
KC = POINTS // KCUT
SEND_AFTER = 2
ROWS = STEPS + DELAYS
COLS = 384
PIECES = 2
WIDTH = MODES // PIECES
SCALE = (MODES * DELAYS) ** -0.5
ORDER = (4, 3, 5, 2, 6, 1, 7)
NARROW = (2, 3, 4, 5, 6)

PLACE = {
    (4, 0): (0, 0),
    (4, 1): (1, 0),
    (3, 0): (3, 0),
    (3, 1): (0, 1),
    (5, 0): (0, 3),
    (5, 1): (1, 1),
    (2, 0): (2, 0),
    (2, 1): (0, 2),
    (6, 0): (1, 3),
    (6, 1): (3, 1),
    (1, 0): (3, 3),
    (1, 1): (2, 1),
    (7, 0): (2, 3),
    (7, 1): (1, 2),
    (0, 0): (3, 2),
    (0, 1): (2, 2),
}
DX = [PLACE[r // 2, r % 2][0] for r in range(16)]
DY = [PLACE[r // 2, r % 2][1] for r in range(16)]
PLANE = sorted(
    ((dx, dy) for dx in range(SIDE) for dy in range(SIDE) if dx or dy),
    key=lambda o: -min(o[0], SIDE - o[0]) - min(o[1], SIDE - o[1]),
)
BACK = [0] * 16
for _r in range(16):
    BACK[DY[_r] * SIDE + DX[_r]] = _r


def lookup(table, index):
    value = jnp.int32(0)
    for at, entry in enumerate(table):
        value = value + jnp.where(index == at, entry, 0)
    return value


def kernel(
    snap,
    pod,
    out,
    sv,
    pv,
    acc,
    sib_buf,
    wide_out,
    wide_in,
    narrow_out,
    narrow_in,
    ci,
    cj,
    s_sem,
    p_sem,
    sib_ss,
    sib_rs,
    rs_ss,
    rs_rs,
    za_ss,
    za_rs,
    sw_ss,
    sw_rs,
    rh_ss,
    rh_rs,
    fw_ss,
    fw_rs,
    sc_ss,
    sc_rs,
    hs_ss,
    hs_rs,
    ag_ss,
    ag_rs,
    ah_ss,
    ah_rs,
):
    def snap_copy(k):
        at = pl.ds(k * KC, KC)
        return pltpu.make_async_copy(snap.at[at], sv.at[at], s_sem.at[k])

    def pod_copy(p, k):
        at = pl.ds(k * KC, KC)
        wide = pl.ds(p * WIDTH, WIDTH)
        return pltpu.make_async_copy(pod.at[at, wide], pv.at[p, at], p_sem.at[p, k])

    for k in range(KCUT):
        snap_copy(k).start()
        pod_copy(0, k).start()
    for p in range(1, PIECES):
        for k in range(KCUT):
            pod_copy(p, k).start()

    space = lax.axis_index("space")
    tm = lax.axis_index("tm")
    z = space // 2
    core = lax.rem(space, 2)
    x = lax.rem(tm, SIDE)
    y = tm // SIDE
    def turn_of(at):
        return at // 2 + lax.rem(at, 2) * (NZ // 2)

    turn = turn_of(z)
    chunk_at = core * NZ + turn

    sibling = {"space": z * 2 + 1 - core, "tm": tm}

    def z_peer(d):
        return {"space": lax.rem(z + d, NZ) * 2 + core, "tm": tm}

    def plane_peer(d):
        dx, dy = PLANE[d]
        return {"space": space, "tm": lax.rem(y + dy, SIDE) * SIDE + lax.rem(x + dx, SIDE)}

    rank = lax.rem(z - tm // 2 + NZ, NZ) * 2 + core
    to_x = lax.rem(x + lookup(DX, rank), SIDE)
    to_y = lax.rem(y + lookup(DY, rank), SIDE)
    scatter_to = {"space": tm, "tm": to_y * SIDE + to_x}
    off_x = lax.rem(x - lax.rem(space, SIDE) + SIDE, SIDE)
    off_y = lax.rem(y - space // SIDE + SIDE, SIDE)
    from_rank = lookup(BACK, off_y * SIDE + off_x)
    from_z = lax.rem(z + from_rank // 2, NZ)
    from_core = lax.rem(from_rank, 2)
    held = from_core * NZ + turn_of(from_z)
    scatter_from = {"space": from_z * 2 + from_core, "tm": space}

    halo_owner = jnp.logical_and(chunk_at < HALO, tm >= 1)
    halo_plane = lax.rem(tm + NT - 1, NT)
    halo_turn = lax.rem(lax.rem(z - halo_plane // 2 + NZ, NZ) // 2 + 2, SIDE)
    halo_to = {"space": halo_plane, "tm": lax.rem(y + halo_turn, SIDE) * SIDE + x}
    has_next = space < NT - 1
    next_block = lax.rem(space + 1, NT)
    holder = jnp.logical_and(has_next, x == lax.rem(next_block, SIDE))
    held_turn = lax.rem(y - next_block // SIDE + 2 + SIDE, SIDE)
    held_halo = lax.rem(z + lax.rem(z, 2) + held_turn * 2, NZ) // 2
    halo_from = {"space": held_halo * 4, "tm": next_block}

    takes_row_halo = tm < NT - 1
    before = lax.rem(tm + NT - 1, NT)
    after = lax.rem(tm + 1, NT)

    barrier = pltpu.get_barrier_semaphore()

    def greet(who):
        pl.semaphore_signal(barrier, inc=1, device_id=who, device_id_type=MESH)

    greet(sibling)
    for d in range(1, NZ):
        greet(z_peer(d))
    for d in range(NT - 1):
        greet(plane_peer(d))
    greet(scatter_from)

    @pl.when(holder)
    def _():
        greet(halo_from)

    @pl.when(jnp.logical_and(core == 0, takes_row_halo))
    def _():
        for k in range(HALO):
            greet({"space": k * 4, "tm": after})

    expected = (
        1
        + (NZ - 1)
        + (NT - 1)
        + 1
        + jnp.where(halo_owner, 1 + NZ, 0)
    )

    cj[:, ROWS:, :] = jnp.zeros((PIECES, COLS - ROWS, WIDTH), jnp.bfloat16)

    @pl.when(jnp.logical_not(has_next))
    def _():
        cj[:, STEPS:ROWS, :] = jnp.zeros((PIECES, DELAYS, WIDTH), jnp.bfloat16)

    @pl.when(jnp.logical_not(takes_row_halo))
    def _():
        ci[:, STEPS:ROWS, :] = jnp.zeros((PIECES, DELAYS, WIDTH), jnp.bfloat16)

    def remote(src, dst, ss, rs, who):
        return pltpu.make_async_remote_copy(
            src_ref=src,
            dst_ref=dst,
            send_sem=ss,
            recv_sem=rs,
            device_id=who,
            device_id_type=MESH,
        )

    def rows_of(start, size):
        return pl.ds(pl.multiple_of(start, CHUNK), size)

    chunk_rows = rows_of(chunk_at * CHUNK, CHUNK)
    held_rows = rows_of(held * CHUNK, CHUNK)
    held_halo_rows = rows_of(STEPS + held_halo * CHUNK, CHUNK)
    own_rows = rows_of(core * OWN, OWN)
    halo_rows = rows_of(STEPS + lax.rem(turn, HALO) * CHUNK, CHUNK)

    def sib_copy(p):
        return remote(
            acc.at[p, rows_of((1 - core) * OWN, OWN)],
            sib_buf.at[p],
            sib_ss.at[p],
            sib_rs.at[p],
            sibling,
        )

    def rs_copy(p, d):
        out_buf, in_buf = (
            (narrow_out, narrow_in) if d in NARROW else (wide_out, wide_in)
        )
        return remote(
            out_buf.at[p, rows_of(turn_of(lax.rem(z + d, NZ)) * CHUNK, CHUNK)],
            in_buf.at[p, d - 1],
            rs_ss.at[p, d - 1],
            rs_rs.at[p, d - 1],
            z_peer(d),
        )

    def za_copy(p, d):
        return remote(
            ci.at[p, chunk_rows],
            ci.at[p, chunk_rows],
            za_ss.at[p, d - 1],
            za_rs.at[p, d - 1],
            z_peer(d),
        )

    def swap_copy(p):
        return remote(
            ci.at[p, own_rows], ci.at[p, own_rows], sw_ss.at[p], sw_rs.at[p], sibling
        )

    def row_halo_copy(p, d):
        return remote(
            ci.at[p, chunk_rows],
            ci.at[p, halo_rows],
            rh_ss.at[p, d],
            rh_rs.at[p, lax.rem(turn, HALO)],
            {"space": lax.rem(z + d, NZ) * 2, "tm": before},
        )

    def row_halo_arrival(p, k):
        at = pl.ds(STEPS + k * CHUNK, CHUNK)
        return pltpu.make_async_copy(ci.at[p, at], ci.at[p, at], rh_rs.at[p, k])

    def forward_copy(p):
        at = pl.ds(STEPS, DELAYS)
        return remote(
            ci.at[p, at], ci.at[p, at], fw_ss.at[p], fw_rs.at[p], sibling
        )

    def scatter_copy(p):
        return remote(
            ci.at[p, chunk_rows],
            cj.at[p, chunk_rows],
            sc_ss.at[p],
            sc_rs.at[p],
            scatter_to,
        )

    def halo_scatter_copy(p):
        return remote(
            ci.at[p, chunk_rows], cj.at[p, halo_rows], hs_ss.at[p], hs_rs.at[p], halo_to
        )

    def ag_copy(p, d):
        return remote(
            cj.at[p, held_rows],
            cj.at[p, held_rows],
            ag_ss.at[p, d],
            ag_rs.at[p, d],
            plane_peer(d),
        )

    def ag_halo_copy(p, d):
        return remote(
            cj.at[p, held_halo_rows],
            cj.at[p, held_halo_rows],
            ah_ss.at[p, d],
            ah_rs.at[p, held_halo],
            plane_peer(d),
        )

    def start_sum(p):
        sib_copy(p).wait_recv()
        both = acc[p, own_rows] + sib_buf[p]
        wide_out[p] = both
        narrow_out[p] = both.astype(jnp.bfloat16)
        for d in ORDER:
            rs_copy(p, d).start()

    def finish_sum(p):
        total = wide_out[p, rows_of(turn * CHUNK, CHUNK)]
        for d in ORDER[::-1]:
            rs_copy(p, d).wait_recv()
            in_buf = narrow_in if d in NARROW else wide_in
            total = total + in_buf[p, d - 1].astype(jnp.float32)
        ci[p, chunk_rows] = total.astype(jnp.bfloat16)
        scatter_copy(p).start()

        @pl.when(halo_owner)
        def _():
            halo_scatter_copy(p).start()

    def start_z(p):
        for d in ORDER:
            za_copy(p, d).start()

        @pl.when(halo_owner)
        def _():
            for d in ORDER + (0,):
                row_halo_copy(p, d).start()

    def start_plane(p):
        scatter_copy(p).wait_recv()
        for d in range(NT - 1):
            ag_copy(p, d).start()

    def start_halo(p):
        @pl.when(holder)
        def _():
            halo_scatter_copy(p).wait_recv()
            for d in range(NT - 1):
                ag_halo_copy(p, d).start()

    def finish_z(p):
        for d in ORDER[::-1]:
            za_copy(p, d).wait_recv()
        swap_copy(p).start()

        @pl.when(jnp.logical_and(core == 0, takes_row_halo))
        def _():
            for k in range(HALO):
                row_halo_arrival(p, k).wait()
            forward_copy(p).start()

    def gram(p):
        swap_copy(p).wait_recv()

        @pl.when(jnp.logical_and(core == 1, takes_row_halo))
        def _():
            forward_copy(p).wait_recv()

        for d in range(NT - 1)[::-1]:
            ag_copy(p, d).wait_recv()
        for k in range(HALO):

            @pl.when(
                jnp.logical_and(
                    has_next, jnp.logical_not(jnp.logical_and(holder, held_halo == k))
                )
            )
            def _():
                pltpu.make_async_copy(
                    cj.at[p, pl.ds(0, CHUNK)],
                    cj.at[p, pl.ds(STEPS + k * CHUNK, CHUNK)],
                    ah_rs.at[p, k],
                ).wait()

        return lax.dot_general(
            ci[p],
            cj[p],
            (((1,), (1,)), ((), ())),
            preferred_element_type=jnp.float32,
        )

    def multiply(p, k):
        if p == 0:
            snap_copy(k).wait()
        pod_copy(p, k).wait()
        at = pl.ds(k * KC, KC)
        for part in range(2):
            rows = slice(part * OWN, (part + 1) * OWN)
            term = lax.dot_general(
                sv[at, rows],
                pv[p, at],
                (((0,), (0,)), ((), ())),
                preferred_element_type=jnp.float32,
            )
            if k == 0:
                acc[p, rows] = term
            else:
                acc[p, rows] += term

    for k in range(KCUT):
        multiply(0, k)
    pl.semaphore_wait(barrier, expected)
    sib_copy(0).start()
    for k in range(KCUT):
        if k == SEND_AFTER:
            start_sum(0)
        multiply(1, k)
    sib_copy(1).start()
    start_sum(1)
    for p in range(PIECES):
        finish_sum(p)
    for p in range(PIECES):
        start_z(p)
    for p in range(PIECES):
        start_plane(p)
        start_halo(p)
    for p in range(PIECES):
        finish_z(p)

    for p in range(PIECES):
        sib_copy(p).wait_send()
        for d in range(1, NZ):
            rs_copy(p, d).wait_send()
            za_copy(p, d).wait_send()
        scatter_copy(p).wait_send()

        @pl.when(halo_owner)
        def _():
            halo_scatter_copy(p).wait_send()
            for d in range(NZ):
                row_halo_copy(p, d).wait_send()

    window = gram(0)
    for p in range(1, PIECES):
        window = window + gram(p)
    shift = 1
    while shift < DELAYS:
        moved = pltpu.roll(window, ROWS - shift, 0)
        window = window + pltpu.roll(moved, COLS - shift, 1)
        shift *= 2
    out[...] = window[:STEPS, :STEPS] * SCALE

    for p in range(PIECES):
        swap_copy(p).wait_send()

        @pl.when(jnp.logical_and(core == 0, takes_row_halo))
        def _():
            forward_copy(p).wait_send()

        for d in range(NT - 1):
            ag_copy(p, d).wait_send()

        @pl.when(holder)
        def _():
            for d in range(NT - 1):
                ag_halo_copy(p, d).wait_send()


def per_device(snapshots, pod_basis):
    dma = pltpu.SemaphoreType.DMA
    f32, bf16 = jnp.float32, jnp.bfloat16
    sems = [dma((KCUT,)), dma((PIECES, KCUT))]
    for sent, received in (
        ((), ()),
        ((NZ - 1,), (NZ - 1,)),
        ((NZ - 1,), (NZ - 1,)),
        ((), ()),
        ((NZ,), (HALO,)),
        ((), ()),
        ((), ()),
        ((), ()),
        ((NT - 1,), (NT - 1,)),
        ((NT - 1,), (4,)),
    ):
        sems += [dma((PIECES,) + sent), dma((PIECES,) + received)]
    return pl.pallas_call(
        kernel,
        out_shape=jax.ShapeDtypeStruct((STEPS, STEPS), f32),
        in_specs=[pl.BlockSpec(memory_space=pl.ANY)] * 2,
        out_specs=pl.BlockSpec(memory_space=pltpu.VMEM),
        scratch_shapes=[
            pltpu.VMEM((POINTS, STEPS), bf16),
            pltpu.VMEM((PIECES, POINTS, WIDTH), bf16),
            pltpu.VMEM((PIECES, STEPS, WIDTH), f32),
            pltpu.VMEM((PIECES, OWN, WIDTH), f32),
            pltpu.VMEM((PIECES, OWN, WIDTH), f32),
            pltpu.VMEM((PIECES, NZ - 1, CHUNK, WIDTH), f32),
            pltpu.VMEM((PIECES, OWN, WIDTH), bf16),
            pltpu.VMEM((PIECES, NZ - 1, CHUNK, WIDTH), bf16),
            pltpu.VMEM((PIECES, ROWS, WIDTH), bf16),
            pltpu.VMEM((PIECES, COLS, WIDTH), bf16),
        ]
        + sems,
        compiler_params=pltpu.CompilerParams(
            collective_id=0, has_side_effects=True, vmem_limit_bytes=50 << 20
        ),
    )(snapshots, pod_basis)


def solution(mesh):
    in_specs = (P("space", "tm"), P("space", None))
    out_specs = P("tm", "space")
    return jax.shard_map(
        per_device, mesh=mesh, in_specs=in_specs, out_specs=out_specs, check_vma=False
    )
```

```python
import jax
import jax.numpy as jnp
from jax import lax
from jax.experimental import pallas as pl
from jax.experimental.pallas import tpu as pltpu
from jax.sharding import PartitionSpec as P

MODES = 512
DELAYS = 64
MESH = pl.DeviceIdType.MESH
NZ = 8
NT = 16
SIDE = 4
STEPS = 256
POINTS = 8192
CHUNK = 16
HALO = DELAYS // CHUNK
OWN = STEPS // 2
KCUT = 4
KC = POINTS // KCUT
SEND_AFTER = 1
ROWS = STEPS + DELAYS
COLS = 384
PIECES = 2
WIDTH = MODES // PIECES
SCALE = (MODES * DELAYS) ** -0.5
ORDER = (4, 3, 5, 2, 6, 1, 7)
NARROW = (2, 3, 4, 5, 6)

PLACE = {
    (4, 0): (0, 0),
    (4, 1): (1, 0),
    (3, 0): (3, 0),
    (3, 1): (0, 1),
    (5, 0): (0, 3),
    (5, 1): (1, 1),
    (2, 0): (2, 0),
    (2, 1): (0, 2),
    (6, 0): (1, 3),
    (6, 1): (3, 1),
    (1, 0): (3, 3),
    (1, 1): (2, 1),
    (7, 0): (2, 3),
    (7, 1): (1, 2),
    (0, 0): (3, 2),
    (0, 1): (2, 2),
}
DX = [PLACE[r // 2, r % 2][0] for r in range(16)]
DY = [PLACE[r // 2, r % 2][1] for r in range(16)]
PLANE = sorted(
    ((dx, dy) for dx in range(SIDE) for dy in range(SIDE) if dx or dy),
    key=lambda o: -min(o[0], SIDE - o[0]) - min(o[1], SIDE - o[1]),
)
BACK = [0] * 16
for _r in range(16):
    BACK[DY[_r] * SIDE + DX[_r]] = _r


def lookup(table, index):
    value = jnp.int32(0)
    for at, entry in enumerate(table):
        value = value + jnp.where(index == at, entry, 0)
    return value


def kernel(
    snap,
    pod,
    out,
    sv,
    pv,
    acc,
    sib_buf,
    wide_out,
    wide_in,
    narrow_out,
    narrow_in,
    ci,
    cj,
    s_sem,
    p_sem,
    sib_ss,
    sib_rs,
    rs_ss,
    rs_rs,
    za_ss,
    za_rs,
    sw_ss,
    sw_rs,
    rh_ss,
    rh_rs,
    fw_ss,
    fw_rs,
    sc_ss,
    sc_rs,
    hs_ss,
    hs_rs,
    ag_ss,
    ag_rs,
    ah_ss,
    ah_rs,
):
    def snap_copy(k):
        at = pl.ds(k * KC, KC)
        return pltpu.make_async_copy(snap.at[at], sv.at[at], s_sem.at[k])

    def pod_copy(p, k):
        at = pl.ds(k * KC, KC)
        wide = pl.ds(p * WIDTH, WIDTH)
        return pltpu.make_async_copy(pod.at[at, wide], pv.at[p, at], p_sem.at[p, k])

    for k in range(KCUT):
        snap_copy(k).start()
        pod_copy(0, k).start()
    for p in range(1, PIECES):
        for k in range(KCUT):
            pod_copy(p, k).start()

    space = lax.axis_index("space")
    tm = lax.axis_index("tm")
    z = space // 2
    core = lax.rem(space, 2)
    x = lax.rem(tm, SIDE)
    y = tm // SIDE
    def turn_of(at):
        return at // 2 + lax.rem(at, 2) * (NZ // 2)

    turn = turn_of(z)
    chunk_at = core * NZ + turn

    sibling = {"space": z * 2 + 1 - core, "tm": tm}

    def z_peer(d):
        return {"space": lax.rem(z + d, NZ) * 2 + core, "tm": tm}

    def plane_peer(d):
        dx, dy = PLANE[d]
        return {"space": space, "tm": lax.rem(y + dy, SIDE) * SIDE + lax.rem(x + dx, SIDE)}

    rank = lax.rem(z - tm // 2 + NZ, NZ) * 2 + core
    to_x = lax.rem(x + lookup(DX, rank), SIDE)
    to_y = lax.rem(y + lookup(DY, rank), SIDE)
    scatter_to = {"space": tm, "tm": to_y * SIDE + to_x}
    off_x = lax.rem(x - lax.rem(space, SIDE) + SIDE, SIDE)
    off_y = lax.rem(y - space // SIDE + SIDE, SIDE)
    from_rank = lookup(BACK, off_y * SIDE + off_x)
    from_z = lax.rem(z + from_rank // 2, NZ)
    from_core = lax.rem(from_rank, 2)
    held = from_core * NZ + turn_of(from_z)
    scatter_from = {"space": from_z * 2 + from_core, "tm": space}

    halo_owner = jnp.logical_and(chunk_at < HALO, tm >= 1)
    halo_plane = lax.rem(tm + NT - 1, NT)
    halo_turn = lax.rem(lax.rem(z - halo_plane // 2 + NZ, NZ) // 2 + 2, SIDE)
    halo_to = {"space": halo_plane, "tm": lax.rem(y + halo_turn, SIDE) * SIDE + x}
    has_next = space < NT - 1
    next_block = lax.rem(space + 1, NT)
    holder = jnp.logical_and(has_next, x == lax.rem(next_block, SIDE))
    held_turn = lax.rem(y - next_block // SIDE + 2 + SIDE, SIDE)
    held_halo = lax.rem(z + lax.rem(z, 2) + held_turn * 2, NZ) // 2
    halo_from = {"space": held_halo * 4, "tm": next_block}

    takes_row_halo = tm < NT - 1
    before = lax.rem(tm + NT - 1, NT)
    after = lax.rem(tm + 1, NT)

    barrier = pltpu.get_barrier_semaphore()

    def greet(who):
        pl.semaphore_signal(barrier, inc=1, device_id=who, device_id_type=MESH)

    greet(sibling)
    for d in range(1, NZ):
        greet(z_peer(d))
    for d in range(NT - 1):
        greet(plane_peer(d))
    greet(scatter_from)

    @pl.when(holder)
    def _():
        greet(halo_from)

    @pl.when(jnp.logical_and(core == 0, takes_row_halo))
    def _():
        for k in range(HALO):
            greet({"space": k * 4, "tm": after})

    expected = (
        1
        + (NZ - 1)
        + (NT - 1)
        + 1
        + jnp.where(halo_owner, 1 + NZ, 0)
    )

    cj[:, ROWS:, :] = jnp.zeros((PIECES, COLS - ROWS, WIDTH), jnp.bfloat16)

    @pl.when(jnp.logical_not(has_next))
    def _():
        cj[:, STEPS:ROWS, :] = jnp.zeros((PIECES, DELAYS, WIDTH), jnp.bfloat16)

    @pl.when(jnp.logical_not(takes_row_halo))
    def _():
        ci[STEPS:ROWS, :] = jnp.zeros((DELAYS, MODES), jnp.bfloat16)

    def remote(src, dst, ss, rs, who):
        return pltpu.make_async_remote_copy(
            src_ref=src,
            dst_ref=dst,
            send_sem=ss,
            recv_sem=rs,
            device_id=who,
            device_id_type=MESH,
        )

    def rows_of(start, size):
        return pl.ds(pl.multiple_of(start, CHUNK), size)

    def wide_of(p):
        return pl.ds(p * WIDTH, WIDTH)

    chunk_rows = rows_of(chunk_at * CHUNK, CHUNK)
    held_rows = rows_of(held * CHUNK, CHUNK)
    held_halo_rows = rows_of(STEPS + held_halo * CHUNK, CHUNK)
    own_rows = rows_of(core * OWN, OWN)
    halo_rows = rows_of(STEPS + lax.rem(turn, HALO) * CHUNK, CHUNK)

    def sib_copy(p):
        return remote(
            acc.at[p, rows_of((1 - core) * OWN, OWN)],
            sib_buf.at[p],
            sib_ss.at[p],
            sib_rs.at[p],
            sibling,
        )

    def rs_copy(p, d):
        out_buf, in_buf = (
            (narrow_out, narrow_in) if d in NARROW else (wide_out, wide_in)
        )
        return remote(
            out_buf.at[p, rows_of(turn_of(lax.rem(z + d, NZ)) * CHUNK, CHUNK)],
            in_buf.at[p, d - 1],
            rs_ss.at[p, d - 1],
            rs_rs.at[p, d - 1],
            z_peer(d),
        )

    def za_copy(d):
        return remote(
            ci.at[chunk_rows],
            ci.at[chunk_rows],
            za_ss.at[d - 1],
            za_rs.at[d - 1],
            z_peer(d),
        )

    def swap_copy():
        return remote(
            ci.at[own_rows], ci.at[own_rows], sw_ss.at[0], sw_rs.at[0], sibling
        )

    def row_halo_copy(d):
        return remote(
            ci.at[chunk_rows],
            ci.at[halo_rows],
            rh_ss.at[d],
            rh_rs.at[lax.rem(turn, HALO)],
            {"space": lax.rem(z + d, NZ) * 2, "tm": before},
        )

    def row_halo_arrival(k):
        at = pl.ds(STEPS + k * CHUNK, CHUNK)
        return pltpu.make_async_copy(ci.at[at], ci.at[at], rh_rs.at[k])

    def forward_copy():
        at = pl.ds(STEPS, DELAYS)
        return remote(
            ci.at[at], ci.at[at], fw_ss.at[0], fw_rs.at[0], sibling
        )

    def scatter_copy(p):
        return remote(
            ci.at[chunk_rows, wide_of(p)],
            cj.at[p, chunk_rows],
            sc_ss.at[p],
            sc_rs.at[p],
            scatter_to,
        )

    def halo_scatter_copy(p):
        return remote(
            ci.at[chunk_rows, wide_of(p)], cj.at[p, halo_rows], hs_ss.at[p], hs_rs.at[p], halo_to
        )

    def ag_copy(p, d):
        return remote(
            cj.at[p, held_rows],
            cj.at[p, held_rows],
            ag_ss.at[p, d],
            ag_rs.at[p, d],
            plane_peer(d),
        )

    def ag_halo_copy(p, d):
        return remote(
            cj.at[p, held_halo_rows],
            cj.at[p, held_halo_rows],
            ah_ss.at[p, d],
            ah_rs.at[p, held_halo],
            plane_peer(d),
        )

    def start_sum(p):
        sib_copy(p).wait_recv()
        both = acc[p, own_rows] + sib_buf[p]
        wide_out[p] = both
        narrow_out[p] = both.astype(jnp.bfloat16)
        for d in ORDER:
            rs_copy(p, d).start()

    def finish_sum(p):
        total = wide_out[p, rows_of(turn * CHUNK, CHUNK)]
        for d in ORDER[::-1]:
            rs_copy(p, d).wait_recv()
            in_buf = narrow_in if d in NARROW else wide_in
            total = total + in_buf[p, d - 1].astype(jnp.float32)
        ci[chunk_rows, wide_of(p)] = total.astype(jnp.bfloat16)
        scatter_copy(p).start()

        @pl.when(halo_owner)
        def _():
            halo_scatter_copy(p).start()

    def start_z():
        for d in ORDER:
            za_copy(d).start()

            @pl.when(halo_owner)
            def _():
                row_halo_copy(d).start()

        @pl.when(halo_owner)
        def _():
            row_halo_copy(0).start()

    def start_plane(p):
        scatter_copy(p).wait_recv()
        for d in range(NT - 1):
            ag_copy(p, d).start()

    def start_halo(p):
        @pl.when(holder)
        def _():
            halo_scatter_copy(p).wait_recv()
            for d in range(NT - 1):
                ag_halo_copy(p, d).start()

    def finish_z():
        for d in ORDER[::-1]:
            za_copy(d).wait_recv()
        swap_copy().start()

        @pl.when(jnp.logical_and(core == 0, takes_row_halo))
        def _():
            for k in range(HALO):
                row_halo_arrival(k).wait()
            forward_copy().start()

    def gram(p):
        for d in range(NT - 1)[::-1]:
            ag_copy(p, d).wait_recv()
        for k in range(HALO):

            @pl.when(
                jnp.logical_and(
                    has_next, jnp.logical_not(jnp.logical_and(holder, held_halo == k))
                )
            )
            def _():
                pltpu.make_async_copy(
                    cj.at[p, pl.ds(0, CHUNK)],
                    cj.at[p, pl.ds(STEPS + k * CHUNK, CHUNK)],
                    ah_rs.at[p, k],
                ).wait()

        return lax.dot_general(
            ci[:, p * WIDTH : (p + 1) * WIDTH],
            cj[p],
            (((1,), (1,)), ((), ())),
            preferred_element_type=jnp.float32,
        )

    def multiply(p, k):
        if p == 0:
            snap_copy(k).wait()
        pod_copy(p, k).wait()
        at = pl.ds(k * KC, KC)
        for part in range(2):
            rows = slice(part * OWN, (part + 1) * OWN)
            term = lax.dot_general(
                sv[at, rows],
                pv[p, at],
                (((0,), (0,)), ((), ())),
                preferred_element_type=jnp.float32,
            )
            if k == 0:
                acc[p, rows] = term
            else:
                acc[p, rows] += term

    for k in range(KCUT):
        multiply(0, k)
    pl.semaphore_wait(barrier, expected)
    sib_copy(0).start()
    for k in range(KCUT):
        if k == SEND_AFTER:
            start_sum(0)
        multiply(1, k)
    sib_copy(1).start()
    start_sum(1)
    for p in range(PIECES):
        finish_sum(p)
    start_z()
    for p in range(PIECES):
        start_plane(p)
        start_halo(p)
    finish_z()

    for p in range(PIECES):
        sib_copy(p).wait_send()
        for d in range(1, NZ):
            rs_copy(p, d).wait_send()
        scatter_copy(p).wait_send()

        @pl.when(halo_owner)
        def _():
            halo_scatter_copy(p).wait_send()

    swap_copy().wait_recv()

    @pl.when(jnp.logical_and(core == 1, takes_row_halo))
    def _():
        forward_copy().wait_recv()

    window = gram(0)

    for d in range(1, NZ):
        za_copy(d).wait_send()

    @pl.when(halo_owner)
    def _():
        for d in range(NZ):
            row_halo_copy(d).wait_send()

    swap_copy().wait_send()

    @pl.when(jnp.logical_and(core == 0, takes_row_halo))
    def _():
        forward_copy().wait_send()

    for p in range(PIECES):
        for d in range(NT - 1):
            ag_copy(p, d).wait_send()

        @pl.when(holder)
        def _():
            for d in range(NT - 1):
                ag_halo_copy(p, d).wait_send()

    for p in range(1, PIECES):
        window = window + gram(p)
    shift = DELAYS // 2
    while shift >= 8:
        rows = window.shape[0] - shift
        moved = pltpu.roll(window[shift:], COLS - shift, 1)
        window = window[:rows] + moved
        shift //= 2
    while shift >= 1:
        moved = pltpu.roll(window, window.shape[0] - shift, 0)
        window = window + pltpu.roll(moved, COLS - shift, 1)
        shift //= 2
    out[...] = window[:STEPS, :STEPS] * SCALE


def per_device(snapshots, pod_basis):
    dma = pltpu.SemaphoreType.DMA
    f32, bf16 = jnp.float32, jnp.bfloat16
    sems = [dma((KCUT,)), dma((PIECES, KCUT))]
    two = (PIECES,)
    for sent, received in (
        (two, two),
        (two + (NZ - 1,), two + (NZ - 1,)),
        ((NZ - 1,), (NZ - 1,)),
        ((1,), (1,)),
        ((NZ,), (HALO,)),
        ((1,), (1,)),
        (two, two),
        (two, two),
        (two + (NT - 1,), two + (NT - 1,)),
        (two + (NT - 1,), two + (HALO,)),
    ):
        sems += [dma(sent), dma(received)]
    return pl.pallas_call(
        kernel,
        out_shape=jax.ShapeDtypeStruct((STEPS, STEPS), f32),
        in_specs=[pl.BlockSpec(memory_space=pl.ANY)] * 2,
        out_specs=pl.BlockSpec(memory_space=pltpu.VMEM),
        scratch_shapes=[
            pltpu.VMEM((POINTS, STEPS), bf16),
            pltpu.VMEM((PIECES, POINTS, WIDTH), bf16),
            pltpu.VMEM((PIECES, STEPS, WIDTH), f32),
            pltpu.VMEM((PIECES, OWN, WIDTH), f32),
            pltpu.VMEM((PIECES, OWN, WIDTH), f32),
            pltpu.VMEM((PIECES, NZ - 1, CHUNK, WIDTH), f32),
            pltpu.VMEM((PIECES, OWN, WIDTH), bf16),
            pltpu.VMEM((PIECES, NZ - 1, CHUNK, WIDTH), bf16),
            pltpu.VMEM((ROWS, MODES), bf16),
            pltpu.VMEM((PIECES, COLS, WIDTH), bf16),
        ]
        + sems,
        compiler_params=pltpu.CompilerParams(
            collective_id=0, has_side_effects=True, vmem_limit_bytes=50 << 20
        ),
    )(snapshots, pod_basis)


def solution(mesh):
    in_specs = (P("space", "tm"), P("space", None))
    out_specs = P("tm", "space")
    return jax.shard_map(
        per_device, mesh=mesh, in_specs=in_specs, out_specs=out_specs, check_vma=False
    )
```

```python
import jax
import jax.numpy as jnp
from jax import lax
from jax.experimental import pallas as pl
from jax.experimental.pallas import tpu as pltpu
from jax.sharding import PartitionSpec as P

MODES = 512
DELAYS = 64
MESH = pl.DeviceIdType.MESH
NZ = 8
NT = 16
SIDE = 4
STEPS = 256
POINTS = 8192
CHUNK = 16
HALO = DELAYS // CHUNK
OWN = STEPS // 2
KCUT = 4
KC = POINTS // KCUT
LOAD_AFTER = 0
SEND_AFTER = 1
ROWS = STEPS + DELAYS
COLS = 384
PIECES = 2
WIDTH = MODES // PIECES
SCALE = (MODES * DELAYS) ** -0.5
ORDER = (4, 3, 5, 2, 6, 1, 7)
NARROW = (2, 3, 4, 5, 6)

PLACE = {
    (4, 0): (0, 0),
    (4, 1): (1, 0),
    (3, 0): (3, 0),
    (3, 1): (0, 1),
    (5, 0): (0, 3),
    (5, 1): (1, 1),
    (2, 0): (2, 0),
    (2, 1): (0, 2),
    (6, 0): (1, 3),
    (6, 1): (3, 1),
    (1, 0): (3, 3),
    (1, 1): (2, 1),
    (7, 0): (2, 3),
    (7, 1): (1, 2),
    (0, 0): (3, 2),
    (0, 1): (2, 2),
}
DX = [PLACE[r // 2, r % 2][0] for r in range(16)]
DY = [PLACE[r // 2, r % 2][1] for r in range(16)]
PLANE = sorted(
    ((dx, dy) for dx in range(SIDE) for dy in range(SIDE) if dx or dy),
    key=lambda o: -min(o[0], SIDE - o[0]) - min(o[1], SIDE - o[1]),
)
BACK = [0] * 16
for _r in range(16):
    BACK[DY[_r] * SIDE + DX[_r]] = _r


def lookup(table, index):
    value = jnp.int32(0)
    for at, entry in enumerate(table):
        value = value + jnp.where(index == at, entry, 0)
    return value


def kernel(
    snap,
    pod,
    out,
    sv,
    pv,
    acc,
    sib_buf,
    wide_out,
    wide_in,
    narrow_out,
    narrow_in,
    ci,
    cj,
    s_sem,
    p_sem,
    sib_ss,
    sib_rs,
    rs_ss,
    rs_rs,
    za_ss,
    za_rs,
    sw_ss,
    sw_rs,
    rh_ss,
    rh_rs,
    fw_ss,
    fw_rs,
    sc_ss,
    sc_rs,
    hs_ss,
    hs_rs,
    ag_ss,
    ag_rs,
    ah_ss,
    ah_rs,
):
    def snap_copy(k):
        at = pl.ds(k * KC, KC)
        return pltpu.make_async_copy(snap.at[at], sv.at[at], s_sem.at[k])

    def pod_copy(p, k):
        at = pl.ds(k * KC, KC)
        wide = pl.ds(p * WIDTH, WIDTH)
        return pltpu.make_async_copy(pod.at[at, wide], pv.at[p, at], p_sem.at[p, k])

    for k in range(KCUT):
        snap_copy(k).start()
        pod_copy(0, k).start()

    space = lax.axis_index("space")
    tm = lax.axis_index("tm")
    z = space // 2
    core = lax.rem(space, 2)
    x = lax.rem(tm, SIDE)
    y = tm // SIDE
    def turn_of(at):
        return at // 2 + lax.rem(at, 2) * (NZ // 2)

    turn = turn_of(z)
    chunk_at = core * NZ + turn

    sibling = {"space": z * 2 + 1 - core, "tm": tm}

    def z_peer(d):
        return {"space": lax.rem(z + d, NZ) * 2 + core, "tm": tm}

    def plane_peer(d):
        dx, dy = PLANE[d]
        return {"space": space, "tm": lax.rem(y + dy, SIDE) * SIDE + lax.rem(x + dx, SIDE)}

    rank = lax.rem(z - tm // 2 + NZ, NZ) * 2 + core
    to_x = lax.rem(x + lookup(DX, rank), SIDE)
    to_y = lax.rem(y + lookup(DY, rank), SIDE)
    scatter_to = {"space": tm, "tm": to_y * SIDE + to_x}
    off_x = lax.rem(x - lax.rem(space, SIDE) + SIDE, SIDE)
    off_y = lax.rem(y - space // SIDE + SIDE, SIDE)
    from_rank = lookup(BACK, off_y * SIDE + off_x)
    from_z = lax.rem(z + from_rank // 2, NZ)
    from_core = lax.rem(from_rank, 2)
    held = from_core * NZ + turn_of(from_z)
    scatter_from = {"space": from_z * 2 + from_core, "tm": space}

    halo_owner = jnp.logical_and(chunk_at < HALO, tm >= 1)
    halo_plane = lax.rem(tm + NT - 1, NT)
    halo_turn = lax.rem(lax.rem(z - halo_plane // 2 + NZ, NZ) // 2 + 2, SIDE)
    halo_to = {"space": halo_plane, "tm": lax.rem(y + halo_turn, SIDE) * SIDE + x}
    has_next = space < NT - 1
    next_block = lax.rem(space + 1, NT)
    holder = jnp.logical_and(has_next, x == lax.rem(next_block, SIDE))
    held_turn = lax.rem(y - next_block // SIDE + 2 + SIDE, SIDE)
    held_halo = lax.rem(z + lax.rem(z, 2) + held_turn * 2, NZ) // 2
    halo_from = {"space": held_halo * 4, "tm": next_block}

    takes_row_halo = tm < NT - 1
    before = lax.rem(tm + NT - 1, NT)
    after = lax.rem(tm + 1, NT)

    barrier = pltpu.get_barrier_semaphore()

    def greet(who):
        pl.semaphore_signal(barrier, inc=1, device_id=who, device_id_type=MESH)

    greet(sibling)
    for d in range(1, NZ):
        greet(z_peer(d))
    for d in range(NT - 1):
        greet(plane_peer(d))
    greet(scatter_from)

    @pl.when(holder)
    def _():
        greet(halo_from)

    @pl.when(jnp.logical_and(core == 0, takes_row_halo))
    def _():
        for k in range(HALO):
            greet({"space": k * 4, "tm": after})

    expected = (
        1
        + (NZ - 1)
        + (NT - 1)
        + 1
        + jnp.where(halo_owner, 1 + NZ, 0)
    )

    cj[:, ROWS:, :] = jnp.zeros((PIECES, COLS - ROWS, WIDTH), jnp.bfloat16)

    @pl.when(jnp.logical_not(has_next))
    def _():
        cj[:, STEPS:ROWS, :] = jnp.zeros((PIECES, DELAYS, WIDTH), jnp.bfloat16)

    @pl.when(jnp.logical_not(takes_row_halo))
    def _():
        ci[STEPS:ROWS, :] = jnp.zeros((DELAYS, MODES), jnp.bfloat16)

    def remote(src, dst, ss, rs, who):
        return pltpu.make_async_remote_copy(
            src_ref=src,
            dst_ref=dst,
            send_sem=ss,
            recv_sem=rs,
            device_id=who,
            device_id_type=MESH,
        )

    def rows_of(start, size):
        return pl.ds(pl.multiple_of(start, CHUNK), size)

    def wide_of(p):
        return pl.ds(p * WIDTH, WIDTH)

    chunk_rows = rows_of(chunk_at * CHUNK, CHUNK)
    held_rows = rows_of(held * CHUNK, CHUNK)
    held_halo_rows = rows_of(STEPS + held_halo * CHUNK, CHUNK)
    own_rows = rows_of(core * OWN, OWN)
    halo_rows = rows_of(STEPS + lax.rem(turn, HALO) * CHUNK, CHUNK)

    def sib_copy(p):
        return remote(
            acc.at[p, rows_of((1 - core) * OWN, OWN)],
            sib_buf.at[p],
            sib_ss.at[p],
            sib_rs.at[p],
            sibling,
        )

    def rs_copy(p, d):
        out_buf, in_buf = (
            (narrow_out, narrow_in) if d in NARROW else (wide_out, wide_in)
        )
        return remote(
            out_buf.at[p, rows_of(turn_of(lax.rem(z + d, NZ)) * CHUNK, CHUNK)],
            in_buf.at[p, d - 1],
            rs_ss.at[p, d - 1],
            rs_rs.at[p, d - 1],
            z_peer(d),
        )

    def za_copy(d):
        return remote(
            ci.at[chunk_rows],
            ci.at[chunk_rows],
            za_ss.at[d - 1],
            za_rs.at[d - 1],
            z_peer(d),
        )

    def swap_copy():
        return remote(
            ci.at[own_rows], ci.at[own_rows], sw_ss.at[0], sw_rs.at[0], sibling
        )

    def row_halo_copy(d):
        return remote(
            ci.at[chunk_rows],
            ci.at[halo_rows],
            rh_ss.at[d],
            rh_rs.at[lax.rem(turn, HALO)],
            {"space": lax.rem(z + d, NZ) * 2, "tm": before},
        )

    def row_halo_arrival(k):
        at = pl.ds(STEPS + k * CHUNK, CHUNK)
        return pltpu.make_async_copy(ci.at[at], ci.at[at], rh_rs.at[k])

    def forward_copy():
        at = pl.ds(STEPS, DELAYS)
        return remote(
            ci.at[at], ci.at[at], fw_ss.at[0], fw_rs.at[0], sibling
        )

    def scatter_copy(p):
        return remote(
            ci.at[chunk_rows, wide_of(p)],
            cj.at[p, chunk_rows],
            sc_ss.at[p],
            sc_rs.at[p],
            scatter_to,
        )

    def halo_scatter_copy(p):
        return remote(
            ci.at[chunk_rows, wide_of(p)], cj.at[p, halo_rows], hs_ss.at[p], hs_rs.at[p], halo_to
        )

    def ag_copy(p, d):
        return remote(
            cj.at[p, held_rows],
            cj.at[p, held_rows],
            ag_ss.at[p, d],
            ag_rs.at[p, d],
            plane_peer(d),
        )

    def ag_halo_copy(p, d):
        return remote(
            cj.at[p, held_halo_rows],
            cj.at[p, held_halo_rows],
            ah_ss.at[p, d],
            ah_rs.at[p, held_halo],
            plane_peer(d),
        )

    def start_sum(p):
        sib_copy(p).wait_recv()
        both = acc[p, own_rows] + sib_buf[p]
        wide_out[p] = both
        narrow_out[p] = both.astype(jnp.bfloat16)
        for d in ORDER:
            rs_copy(p, d).start()

    def finish_sum(p):
        total = wide_out[p, rows_of(turn * CHUNK, CHUNK)]
        for d in ORDER[::-1]:
            rs_copy(p, d).wait_recv()
            in_buf = narrow_in if d in NARROW else wide_in
            total = total + in_buf[p, d - 1].astype(jnp.float32)
        ci[chunk_rows, wide_of(p)] = total.astype(jnp.bfloat16)
        scatter_copy(p).start()

        @pl.when(halo_owner)
        def _():
            halo_scatter_copy(p).start()

    def start_z():
        for d in ORDER:
            za_copy(d).start()

            @pl.when(halo_owner)
            def _():
                row_halo_copy(d).start()

        @pl.when(halo_owner)
        def _():
            row_halo_copy(0).start()

    def start_plane(p):
        scatter_copy(p).wait_recv()
        for d in range(NT - 1):
            ag_copy(p, d).start()

    def start_halo(p):
        @pl.when(holder)
        def _():
            halo_scatter_copy(p).wait_recv()
            for d in range(NT - 1):
                ag_halo_copy(p, d).start()

    def finish_z():
        for d in ORDER[::-1]:
            za_copy(d).wait_recv()
        swap_copy().start()

        @pl.when(jnp.logical_and(core == 0, takes_row_halo))
        def _():
            for k in range(HALO):
                row_halo_arrival(k).wait()
            forward_copy().start()

    def gram(p):
        for d in range(NT - 1)[::-1]:
            ag_copy(p, d).wait_recv()
        for k in range(HALO):

            @pl.when(
                jnp.logical_and(
                    has_next, jnp.logical_not(jnp.logical_and(holder, held_halo == k))
                )
            )
            def _():
                pltpu.make_async_copy(
                    cj.at[p, pl.ds(0, CHUNK)],
                    cj.at[p, pl.ds(STEPS + k * CHUNK, CHUNK)],
                    ah_rs.at[p, k],
                ).wait()

        return lax.dot_general(
            ci[:, p * WIDTH : (p + 1) * WIDTH],
            cj[p],
            (((1,), (1,)), ((), ())),
            preferred_element_type=jnp.float32,
        )

    def multiply(p, k):
        if p == 0:
            snap_copy(k).wait()
        pod_copy(p, k).wait()
        at = pl.ds(k * KC, KC)
        for part in range(2):
            rows = slice(part * OWN, (part + 1) * OWN)
            term = lax.dot_general(
                sv[at, rows],
                pv[p, at],
                (((0,), (0,)), ((), ())),
                preferred_element_type=jnp.float32,
            )
            if k == 0:
                acc[p, rows] = term
            else:
                acc[p, rows] += term

    for k in range(KCUT):
        multiply(0, k)
        if k == LOAD_AFTER:
            for later in range(KCUT):
                pod_copy(1, later).start()
    pl.semaphore_wait(barrier, expected)
    sib_copy(0).start()
    for k in range(KCUT):
        if k == SEND_AFTER:
            start_sum(0)
        multiply(1, k)
    sib_copy(1).start()
    start_sum(1)
    for p in range(PIECES):
        finish_sum(p)
    start_z()
    for p in range(PIECES):
        start_plane(p)
        start_halo(p)
    finish_z()

    for p in range(PIECES):
        sib_copy(p).wait_send()
        for d in range(1, NZ):
            rs_copy(p, d).wait_send()
        scatter_copy(p).wait_send()

        @pl.when(halo_owner)
        def _():
            halo_scatter_copy(p).wait_send()

    swap_copy().wait_recv()

    @pl.when(jnp.logical_and(core == 1, takes_row_halo))
    def _():
        forward_copy().wait_recv()

    window = gram(0)

    for d in range(1, NZ):
        za_copy(d).wait_send()

    @pl.when(halo_owner)
    def _():
        for d in range(NZ):
            row_halo_copy(d).wait_send()

    swap_copy().wait_send()

    @pl.when(jnp.logical_and(core == 0, takes_row_halo))
    def _():
        forward_copy().wait_send()

    for p in range(PIECES):
        for d in range(NT - 1):
            ag_copy(p, d).wait_send()

        @pl.when(holder)
        def _():
            for d in range(NT - 1):
                ag_halo_copy(p, d).wait_send()

    for p in range(1, PIECES):
        window = window + gram(p)
    shift = DELAYS // 2
    while shift >= 8:
        rows = window.shape[0] - shift
        moved = pltpu.roll(window[shift:], COLS - shift, 1)
        window = window[:rows] + moved
        shift //= 2
    while shift >= 1:
        moved = pltpu.roll(window, window.shape[0] - shift, 0)
        window = window + pltpu.roll(moved, COLS - shift, 1)
        shift //= 2
    out[...] = window[:STEPS, :STEPS] * SCALE


def per_device(snapshots, pod_basis):
    dma = pltpu.SemaphoreType.DMA
    f32, bf16 = jnp.float32, jnp.bfloat16
    sems = [dma((KCUT,)), dma((PIECES, KCUT))]
    two = (PIECES,)
    for sent, received in (
        (two, two),
        (two + (NZ - 1,), two + (NZ - 1,)),
        ((NZ - 1,), (NZ - 1,)),
        ((1,), (1,)),
        ((NZ,), (HALO,)),
        ((1,), (1,)),
        (two, two),
        (two, two),
        (two + (NT - 1,), two + (NT - 1,)),
        (two + (NT - 1,), two + (HALO,)),
    ):
        sems += [dma(sent), dma(received)]
    return pl.pallas_call(
        kernel,
        out_shape=jax.ShapeDtypeStruct((STEPS, STEPS), f32),
        in_specs=[pl.BlockSpec(memory_space=pl.ANY)] * 2,
        out_specs=pl.BlockSpec(memory_space=pltpu.VMEM),
        scratch_shapes=[
            pltpu.VMEM((POINTS, STEPS), bf16),
            pltpu.VMEM((PIECES, POINTS, WIDTH), bf16),
            pltpu.VMEM((PIECES, STEPS, WIDTH), f32),
            pltpu.VMEM((PIECES, OWN, WIDTH), f32),
            pltpu.VMEM((PIECES, OWN, WIDTH), f32),
            pltpu.VMEM((PIECES, NZ - 1, CHUNK, WIDTH), f32),
            pltpu.VMEM((PIECES, OWN, WIDTH), bf16),
            pltpu.VMEM((PIECES, NZ - 1, CHUNK, WIDTH), bf16),
            pltpu.VMEM((ROWS, MODES), bf16),
            pltpu.VMEM((PIECES, COLS, WIDTH), bf16),
        ]
        + sems,
        compiler_params=pltpu.CompilerParams(
            collective_id=0, has_side_effects=True, vmem_limit_bytes=50 << 20
        ),
    )(snapshots, pod_basis)


def solution(mesh):
    in_specs = (P("space", "tm"), P("space", None))
    out_specs = P("tm", "space")
    return jax.shard_map(
        per_device, mesh=mesh, in_specs=in_specs, out_specs=out_specs, check_vma=False
    )
```

```python
import jax
import jax.numpy as jnp
from jax import lax
from jax.experimental import pallas as pl
from jax.experimental.pallas import tpu as pltpu
from jax.sharding import PartitionSpec as P

MODES = 512
DELAYS = 64
MESH = pl.DeviceIdType.MESH
NZ = 8
NT = 16
SIDE = 4
STEPS = 256
POINTS = 8192
CHUNK = 16
HALO = DELAYS // CHUNK
OWN = STEPS // 2
KCUT = 4
KC = POINTS // KCUT
LOAD_AFTER = 0
SEND_AFTER = 1
ROWS = STEPS + DELAYS
COLS = 384
PIECES = 2
WIDTH = MODES // PIECES
SCALE = (MODES * DELAYS) ** -0.5
ORDER = (4, 3, 5, 2, 6, 1, 7)
NARROW = (2, 3, 4, 5, 6)

PLACE = {
    (4, 0): (0, 0),
    (4, 1): (1, 0),
    (3, 0): (3, 0),
    (3, 1): (0, 1),
    (5, 0): (0, 3),
    (5, 1): (1, 1),
    (2, 0): (2, 0),
    (2, 1): (0, 2),
    (6, 0): (1, 3),
    (6, 1): (3, 1),
    (1, 0): (3, 3),
    (1, 1): (2, 1),
    (7, 0): (2, 3),
    (7, 1): (1, 2),
    (0, 0): (3, 2),
    (0, 1): (2, 2),
}
DX = [PLACE[r // 2, r % 2][0] for r in range(16)]
DY = [PLACE[r // 2, r % 2][1] for r in range(16)]
PLANE = sorted(
    ((dx, dy) for dx in range(SIDE) for dy in range(SIDE) if dx or dy),
    key=lambda o: -min(o[0], SIDE - o[0]) - min(o[1], SIDE - o[1]),
)
BACK = [0] * 16
for _r in range(16):
    BACK[DY[_r] * SIDE + DX[_r]] = _r


def lookup(table, index):
    value = jnp.int32(0)
    for at, entry in enumerate(table):
        value = value + jnp.where(index == at, entry, 0)
    return value


def kernel(
    snap,
    pod,
    out,
    sv,
    pv,
    acc,
    sib_buf,
    wide_out,
    wide_in,
    narrow_out,
    narrow_in,
    ci,
    cj,
    s_sem,
    p_sem,
    sib_ss,
    sib_rs,
    rs_ss,
    rs_rs,
    za_ss,
    za_rs,
    sw_ss,
    sw_rs,
    rh_ss,
    rh_rs,
    fw_ss,
    fw_rs,
    sc_ss,
    sc_rs,
    hs_ss,
    hs_rs,
    ag_ss,
    ag_rs,
    ah_ss,
    ah_rs,
):
    def snap_copy(k):
        at = pl.ds(k * KC, KC)
        return pltpu.make_async_copy(snap.at[at], sv.at[at], s_sem.at[k])

    def pod_copy(p, k):
        at = pl.ds(k * KC, KC)
        wide = pl.ds(p * WIDTH, WIDTH)
        return pltpu.make_async_copy(pod.at[at, wide], pv.at[p, at], p_sem.at[p, k])

    for k in range(KCUT):
        snap_copy(k).start()
        pod_copy(0, k).start()

    space = lax.axis_index("space")
    tm = lax.axis_index("tm")
    z = space // 2
    core = lax.rem(space, 2)
    x = lax.rem(tm, SIDE)
    y = tm // SIDE
    def turn_of(at):
        return at // 2 + lax.rem(at, 2) * (NZ // 2)

    turn = turn_of(z)
    chunk_at = core * NZ + turn

    sibling = {"space": z * 2 + 1 - core, "tm": tm}

    def z_peer(d):
        return {"space": lax.rem(z + d, NZ) * 2 + core, "tm": tm}

    def plane_peer(d):
        dx, dy = PLANE[d]
        return {"space": space, "tm": lax.rem(y + dy, SIDE) * SIDE + lax.rem(x + dx, SIDE)}

    rank = lax.rem(z - tm // 2 + NZ, NZ) * 2 + core
    to_x = lax.rem(x + lookup(DX, rank), SIDE)
    to_y = lax.rem(y + lookup(DY, rank), SIDE)
    scatter_to = {"space": tm, "tm": to_y * SIDE + to_x}
    off_x = lax.rem(x - lax.rem(space, SIDE) + SIDE, SIDE)
    off_y = lax.rem(y - space // SIDE + SIDE, SIDE)
    from_rank = lookup(BACK, off_y * SIDE + off_x)
    from_z = lax.rem(z + from_rank // 2, NZ)
    from_core = lax.rem(from_rank, 2)
    held = from_core * NZ + turn_of(from_z)
    scatter_from = {"space": from_z * 2 + from_core, "tm": space}

    halo_owner = jnp.logical_and(chunk_at < HALO, tm >= 1)
    halo_plane = lax.rem(tm + NT - 1, NT)
    halo_turn = lax.rem(lax.rem(z - halo_plane // 2 + NZ, NZ) // 2 + 2, SIDE)
    halo_to = {"space": halo_plane, "tm": lax.rem(y + halo_turn, SIDE) * SIDE + x}
    has_next = space < NT - 1
    next_block = lax.rem(space + 1, NT)
    holder = jnp.logical_and(has_next, x == lax.rem(next_block, SIDE))
    held_turn = lax.rem(y - next_block // SIDE + 2 + SIDE, SIDE)
    held_halo = lax.rem(z + lax.rem(z, 2) + held_turn * 2, NZ) // 2
    halo_from = {"space": held_halo * 4, "tm": next_block}

    takes_row_halo = tm < NT - 1
    before = lax.rem(tm + NT - 1, NT)
    after = lax.rem(tm + 1, NT)

    barrier = pltpu.get_barrier_semaphore()

    def greet(who):
        pl.semaphore_signal(barrier, inc=1, device_id=who, device_id_type=MESH)

    greet(sibling)
    for d in range(1, NZ):
        greet(z_peer(d))
    for d in range(NT - 1):
        greet(plane_peer(d))
    greet(scatter_from)

    @pl.when(holder)
    def _():
        greet(halo_from)

    @pl.when(jnp.logical_and(core == 0, takes_row_halo))
    def _():
        for k in range(HALO):
            greet({"space": k * 4, "tm": after})

    expected = (
        1
        + (NZ - 1)
        + (NT - 1)
        + 1
        + jnp.where(halo_owner, 1 + NZ, 0)
    )

    cj[:, ROWS:, :] = jnp.zeros((PIECES, COLS - ROWS, WIDTH), jnp.bfloat16)

    @pl.when(jnp.logical_not(has_next))
    def _():
        cj[:, STEPS:ROWS, :] = jnp.zeros((PIECES, DELAYS, WIDTH), jnp.bfloat16)

    @pl.when(jnp.logical_not(takes_row_halo))
    def _():
        ci[STEPS:ROWS, :] = jnp.zeros((DELAYS, MODES), jnp.bfloat16)

    def remote(src, dst, ss, rs, who):
        return pltpu.make_async_remote_copy(
            src_ref=src,
            dst_ref=dst,
            send_sem=ss,
            recv_sem=rs,
            device_id=who,
            device_id_type=MESH,
        )

    def rows_of(start, size):
        return pl.ds(pl.multiple_of(start, CHUNK), size)

    def wide_of(p):
        return pl.ds(p * WIDTH, WIDTH)

    chunk_rows = rows_of(chunk_at * CHUNK, CHUNK)
    held_rows = rows_of(held * CHUNK, CHUNK)
    held_halo_rows = rows_of(STEPS + held_halo * CHUNK, CHUNK)
    own_rows = rows_of(core * OWN, OWN)
    halo_rows = rows_of(STEPS + lax.rem(turn, HALO) * CHUNK, CHUNK)

    def sib_copy(p):
        return remote(
            acc.at[p, rows_of((1 - core) * OWN, OWN)],
            sib_buf.at[p],
            sib_ss.at[p],
            sib_rs.at[p],
            sibling,
        )

    def rs_copy(p, d):
        out_buf, in_buf = (
            (narrow_out, narrow_in) if d in NARROW else (wide_out, wide_in)
        )
        return remote(
            out_buf.at[p, rows_of(turn_of(lax.rem(z + d, NZ)) * CHUNK, CHUNK)],
            in_buf.at[p, d - 1],
            rs_ss.at[p, d - 1],
            rs_rs.at[p, d - 1],
            z_peer(d),
        )

    def za_copy(d):
        return remote(
            ci.at[chunk_rows],
            ci.at[chunk_rows],
            za_ss.at[d - 1],
            za_rs.at[d - 1],
            z_peer(d),
        )

    def swap_copy(d):
        at = turn_of(lax.rem(z + NZ - d, NZ))
        rows = rows_of((core * NZ + at) * CHUNK, CHUNK)
        return remote(ci.at[rows], ci.at[rows], sw_ss.at[d], sw_rs.at[d], sibling)

    def row_halo_copy(d):
        return remote(
            ci.at[chunk_rows],
            ci.at[halo_rows],
            rh_ss.at[d],
            rh_rs.at[lax.rem(turn, HALO)],
            {"space": lax.rem(z + d, NZ) * 2, "tm": before},
        )

    def row_halo_arrival(k):
        at = pl.ds(STEPS + k * CHUNK, CHUNK)
        return pltpu.make_async_copy(ci.at[at], ci.at[at], rh_rs.at[k])

    def forward_copy():
        at = pl.ds(STEPS, DELAYS)
        return remote(
            ci.at[at], ci.at[at], fw_ss.at[0], fw_rs.at[0], sibling
        )

    def scatter_copy(p):
        return remote(
            ci.at[chunk_rows, wide_of(p)],
            cj.at[p, chunk_rows],
            sc_ss.at[p],
            sc_rs.at[p],
            scatter_to,
        )

    def halo_scatter_copy(p):
        return remote(
            ci.at[chunk_rows, wide_of(p)], cj.at[p, halo_rows], hs_ss.at[p], hs_rs.at[p], halo_to
        )

    def ag_copy(p, d):
        return remote(
            cj.at[p, held_rows],
            cj.at[p, held_rows],
            ag_ss.at[p, d],
            ag_rs.at[p, d],
            plane_peer(d),
        )

    def ag_halo_copy(p, d):
        return remote(
            cj.at[p, held_halo_rows],
            cj.at[p, held_halo_rows],
            ah_ss.at[p, d],
            ah_rs.at[p, held_halo],
            plane_peer(d),
        )

    def start_sum(p):
        sib_copy(p).wait_recv()
        both = acc[p, own_rows] + sib_buf[p]
        wide_out[p] = both
        narrow_out[p] = both.astype(jnp.bfloat16)
        for d in ORDER:
            rs_copy(p, d).start()

    def finish_sum(p):
        total = wide_out[p, rows_of(turn * CHUNK, CHUNK)]
        for d in ORDER[::-1]:
            rs_copy(p, d).wait_recv()
            in_buf = narrow_in if d in NARROW else wide_in
            total = total + in_buf[p, d - 1].astype(jnp.float32)
        ci[chunk_rows, wide_of(p)] = total.astype(jnp.bfloat16)
        scatter_copy(p).start()

        @pl.when(halo_owner)
        def _():
            halo_scatter_copy(p).start()

    def start_z():
        for d in ORDER:
            za_copy(d).start()

            @pl.when(halo_owner)
            def _():
                row_halo_copy(d).start()

        @pl.when(halo_owner)
        def _():
            row_halo_copy(0).start()

    def start_plane(p):
        scatter_copy(p).wait_recv()
        for d in range(NT - 1):
            ag_copy(p, d).start()

    def start_halo(p):
        @pl.when(holder)
        def _():
            halo_scatter_copy(p).wait_recv()
            for d in range(NT - 1):
                ag_halo_copy(p, d).start()

    def finish_z():
        swap_copy(0).start()
        for d in ORDER[::-1]:
            za_copy(d).wait_recv()
            swap_copy(d).start()

        @pl.when(jnp.logical_and(core == 0, takes_row_halo))
        def _():
            for k in range(HALO):
                row_halo_arrival(k).wait()
            forward_copy().start()

    def gram(p):
        for d in range(NT - 1)[::-1]:
            ag_copy(p, d).wait_recv()
        for k in range(HALO):

            @pl.when(
                jnp.logical_and(
                    has_next, jnp.logical_not(jnp.logical_and(holder, held_halo == k))
                )
            )
            def _():
                pltpu.make_async_copy(
                    cj.at[p, pl.ds(0, CHUNK)],
                    cj.at[p, pl.ds(STEPS + k * CHUNK, CHUNK)],
                    ah_rs.at[p, k],
                ).wait()

        return lax.dot_general(
            ci[:, p * WIDTH : (p + 1) * WIDTH],
            cj[p],
            (((1,), (1,)), ((), ())),
            preferred_element_type=jnp.float32,
        )

    def multiply(p, k):
        if p == 0:
            snap_copy(k).wait()
        pod_copy(p, k).wait()
        at = pl.ds(k * KC, KC)
        for part in range(2):
            rows = slice(part * OWN, (part + 1) * OWN)
            term = lax.dot_general(
                sv[at, rows],
                pv[p, at],
                (((0,), (0,)), ((), ())),
                preferred_element_type=jnp.float32,
            )
            if k == 0:
                acc[p, rows] = term
            else:
                acc[p, rows] += term

    for k in range(KCUT):
        multiply(0, k)
        if k == LOAD_AFTER:
            for later in range(KCUT):
                pod_copy(1, later).start()
    pl.semaphore_wait(barrier, expected)
    sib_copy(0).start()
    for k in range(KCUT):
        if k == SEND_AFTER:
            start_sum(0)
        multiply(1, k)
    sib_copy(1).start()
    start_sum(1)
    for p in range(PIECES):
        finish_sum(p)
    start_z()
    for p in range(PIECES):
        start_plane(p)
        start_halo(p)
    finish_z()

    for p in range(PIECES):
        sib_copy(p).wait_send()
        for d in range(1, NZ):
            rs_copy(p, d).wait_send()
        scatter_copy(p).wait_send()

        @pl.when(halo_owner)
        def _():
            halo_scatter_copy(p).wait_send()

    for d in range(NZ):
        swap_copy(d).wait_recv()

    @pl.when(jnp.logical_and(core == 1, takes_row_halo))
    def _():
        forward_copy().wait_recv()

    window = gram(0)

    for d in range(1, NZ):
        za_copy(d).wait_send()

    @pl.when(halo_owner)
    def _():
        for d in range(NZ):
            row_halo_copy(d).wait_send()

    for d in range(NZ):
        swap_copy(d).wait_send()

    @pl.when(jnp.logical_and(core == 0, takes_row_halo))
    def _():
        forward_copy().wait_send()

    for p in range(PIECES):
        for d in range(NT - 1):
            ag_copy(p, d).wait_send()

        @pl.when(holder)
        def _():
            for d in range(NT - 1):
                ag_halo_copy(p, d).wait_send()

    for p in range(1, PIECES):
        window = window + gram(p)
    shift = DELAYS // 2
    while shift >= 8:
        rows = window.shape[0] - shift
        moved = pltpu.roll(window[shift:], COLS - shift, 1)
        window = window[:rows] + moved
        shift //= 2
    while shift >= 1:
        moved = pltpu.roll(window, window.shape[0] - shift, 0)
        window = window + pltpu.roll(moved, COLS - shift, 1)
        shift //= 2
    out[...] = window[:STEPS, :STEPS] * SCALE


def per_device(snapshots, pod_basis):
    dma = pltpu.SemaphoreType.DMA
    f32, bf16 = jnp.float32, jnp.bfloat16
    sems = [dma((KCUT,)), dma((PIECES, KCUT))]
    two = (PIECES,)
    for sent, received in (
        (two, two),
        (two + (NZ - 1,), two + (NZ - 1,)),
        ((NZ - 1,), (NZ - 1,)),
        ((NZ,), (NZ,)),
        ((NZ,), (HALO,)),
        ((1,), (1,)),
        (two, two),
        (two, two),
        (two + (NT - 1,), two + (NT - 1,)),
        (two + (NT - 1,), two + (HALO,)),
    ):
        sems += [dma(sent), dma(received)]
    return pl.pallas_call(
        kernel,
        out_shape=jax.ShapeDtypeStruct((STEPS, STEPS), f32),
        in_specs=[pl.BlockSpec(memory_space=pl.ANY)] * 2,
        out_specs=pl.BlockSpec(memory_space=pltpu.VMEM),
        scratch_shapes=[
            pltpu.VMEM((POINTS, STEPS), bf16),
            pltpu.VMEM((PIECES, POINTS, WIDTH), bf16),
            pltpu.VMEM((PIECES, STEPS, WIDTH), f32),
            pltpu.VMEM((PIECES, OWN, WIDTH), f32),
            pltpu.VMEM((PIECES, OWN, WIDTH), f32),
            pltpu.VMEM((PIECES, NZ - 1, CHUNK, WIDTH), f32),
            pltpu.VMEM((PIECES, OWN, WIDTH), bf16),
            pltpu.VMEM((PIECES, NZ - 1, CHUNK, WIDTH), bf16),
            pltpu.VMEM((ROWS, MODES), bf16),
            pltpu.VMEM((PIECES, COLS, WIDTH), bf16),
        ]
        + sems,
        compiler_params=pltpu.CompilerParams(
            collective_id=0, has_side_effects=True, vmem_limit_bytes=50 << 20
        ),
    )(snapshots, pod_basis)


def solution(mesh):
    in_specs = (P("space", "tm"), P("space", None))
    out_specs = P("tm", "space")
    return jax.shard_map(
        per_device, mesh=mesh, in_specs=in_specs, out_specs=out_specs, check_vma=False
    )
```
